128 devices in a mesh: gx: 8 (over z, x_hi), gy: 4 (over x_lo, core), gz: 4 (over y).
Axes of the slice: x: 4 (x_hi: 2, x_lo: 2; x = x_hi * 2 + x_lo), y: 4, z: 4, core: 2. Of those that a mesh axis runs over, the one named last changes fastest.
Arguments:
- h_blocks: bfloat16 [8, 4, 4, 2, 48, 128, 128], P('gx', 'gy', 'gz'), may hold values from -0.0546875 to 0.0546875
- neighbours: int32 [8, 4, 4, 2, 48], P('gx', 'gy', 'gz'), may hold values from 0 to 53, as said below
- block_counts: int32 [8, 4, 4], P('gx', 'gy', 'gz'), may hold values from 1 to 2, as said below
- cheb_prev_in: bfloat16 [8, 4, 4, 2, 128, 128], P('gx', 'gy', 'gz'), may hold values from -6 to 6
- cheb_curr_in: bfloat16 [8, 4, 4, 2, 128, 128], P('gx', 'gy', 'gz'), may hold values from -6 to 6
- density_in: float32 [8, 4, 4, 2, 128, 128], P('gx', 'gy', 'gz'), may hold values from -6 to 6
- cheb_coeffs: float32 [2], replicated, may hold values from 0.2 to 1
Outputs:
- cheb_mid: bfloat16 [8, 4, 4, 2, 128, 128], P('gx', 'gy', 'gz')
- cheb_next: bfloat16 [8, 4, 4, 2, 128, 128], P('gx', 'gy', 'gz')
- density_out: float32 [8, 4, 4, 2, 128, 128], P('gx', 'gy', 'gz')
The draws below stay inside these ranges and needn't reach their ends.
Inputs may be any that keep to these rules, and one draw needn't show every extreme that they name: `neighbours`: each row block lists 48 distinct entries. `block_counts`: cells in the first and last layers along the slab normal hold 1 block.
All inputs are finite; a program needn't handle non-finite values.
Results may differ from the reference program's by a relative error of at most 0.005.
Values may be sent and summed in bfloat16 or wider, within the bound.
A program may use at most 64 MiB of HBM per device.

```python
import jax
import jax.numpy as jnp
from jax import lax

OB = 128
BMAX = 2
K = 48
PROBES = 128
CX = 8
CY = 4
CZ = 4


def draw_block_counts(key, part):
    key = jax.random.fold_in(key, 1)
    inner_key, outer_key = jax.random.split(key)
    inner = jax.random.randint(inner_key, (CX, CY, CZ), 1, BMAX + 1)
    outer = jax.random.randint(outer_key, (CX, CY, CZ), 1, max(BMAX // 2, 1) + 1)
    layer = jnp.arange(CZ, dtype=jnp.int32)[None, None, :]
    vacuum = (layer == 0) | (layer == CZ - 1)
    counts = jnp.where(vacuum, outer, inner)
    counts = counts.at[0, 0, CZ // 2].set(BMAX)
    return counts.astype(jnp.int32)


def draw_neighbours(key, part):
    key = jax.random.fold_in(key, 2)
    rows = CX * CY * CZ * BMAX
    row_keys = jax.random.split(key, rows)
    lists = jax.vmap(lambda row_key: jax.random.permutation(row_key, 27 * BMAX)[:K])(row_keys)
    first = jnp.concatenate([jnp.array([27 * BMAX - 1], dtype=jnp.int32), jnp.arange(K - 1, dtype=jnp.int32)])
    lists = lists.astype(jnp.int32).at[0].set(first)
    return lists.reshape(CX, CY, CZ, BMAX, K)


def shard_levels(own_key, extent, shards, smallest, high):
    factor_of = 1.0
    for position, shards_of in shards:
        draws = jax.random.uniform(jax.random.fold_in(jax.random.fold_in(own_key, 6), position), (shards_of,), jnp.float32, smallest / len(shards), high / len(shards))
        factor_of = factor_of * jnp.repeat(jnp.exp(draws), extent[position] // shards_of).reshape((-1,) + (1,) * (len(extent) - 1 - position))
    return factor_of


def gaussian(key, shape, spread, reach, cuts=(), kind=jnp.bfloat16):
    drawn = spread * jax.random.normal(key, shape, jnp.float32)
    if cuts:
        drawn = drawn * shard_levels(key, shape, cuts, -0.22, 0.18)
    return jnp.clip(drawn, -reach, reach).astype(kind)


def setup_inputs(seed: int = 0) -> dict:
    keys = jax.random.split(jax.random.key(seed), 8)
    h_blocks = gaussian(keys[0], (CX, CY, CZ, BMAX, K, OB, OB), (2 * K * OB) ** -0.5, 0.0546875, ((0, 8), (1, 4), (2, 4)))
    neighbours = draw_neighbours(jax.random.fold_in(keys[7], 71), 0)
    block_counts = draw_block_counts(jax.random.fold_in(keys[7], 71), 0)
    cheb_prev_in = gaussian(keys[3], (CX, CY, CZ, BMAX, OB, PROBES), 1.0, 6.0, ((0, 8), (1, 4), (2, 4)))
    cheb_curr_in = gaussian(keys[4], (CX, CY, CZ, BMAX, OB, PROBES), 1.0, 6.0, ((0, 8), (1, 4), (2, 4)))
    density_in = gaussian(keys[5], (CX, CY, CZ, BMAX, OB, PROBES), 1.0, 6.0, ((0, 8), (1, 4), (2, 4)), jnp.float32)
    cheb_coeffs = jnp.clip(jax.random.uniform(keys[6], (2,), jnp.float32, 0.2, 1.0), 0.2, 1.0)
    return {"h_blocks": h_blocks, "neighbours": neighbours, "block_counts": block_counts, "cheb_prev_in": cheb_prev_in, "cheb_curr_in": cheb_curr_in, "density_in": density_in, "cheb_coeffs": cheb_coeffs}


def hamiltonian_apply(h_blocks, neighbours, vectors):
    offsets = jnp.arange(27, dtype=jnp.int32)
    shift_x = offsets // 9 - 1
    shift_y = (offsets // 3) % 3 - 1
    shift_z = offsets % 3 - 1

    def one_cell(cell):
        cell_x = cell // (CY * CZ)
        cell_y = (cell // CZ) % CY
        cell_z = cell % CZ
        near_x = (cell_x + shift_x) % CX
        near_y = (cell_y + shift_y) % CY
        near_z = (cell_z + shift_z) % CZ
        beside_all = vectors[near_x, near_y, near_z].reshape(27 * BMAX, OB, PROBES)
        listed = neighbours[cell_x, cell_y, cell_z].reshape(-1)
        picked = jnp.take(beside_all, listed, axis=0).reshape(BMAX, K, OB, PROBES)
        couplings = h_blocks[cell_x, cell_y, cell_z]
        return jnp.einsum("rkab,rkbm->ram", couplings.astype(jnp.float32), picked.astype(jnp.float32))

    cells = jnp.arange(CX * CY * CZ, dtype=jnp.int32)
    result = lax.map(one_cell, cells)
    return result.reshape(CX, CY, CZ, BMAX, OB, PROBES)


def reference(h_blocks, neighbours, block_counts, cheb_prev_in, cheb_curr_in, density_in, cheb_coeffs):
    slot_ids = jnp.arange(BMAX, dtype=jnp.int32)
    live_rows = (slot_ids[None, None, None, :] < block_counts[..., None]).astype(jnp.float32)[..., None, None]
    live_half = live_rows.astype(jnp.bfloat16)
    prev = cheb_prev_in * live_half
    curr = cheb_curr_in * live_half
    cheb_mid = ((2.0 * hamiltonian_apply(h_blocks, neighbours, curr) - prev.astype(jnp.float32)) * live_rows).astype(jnp.bfloat16)
    cheb_next = ((2.0 * hamiltonian_apply(h_blocks, neighbours, cheb_mid) - curr.astype(jnp.float32)) * live_rows).astype(jnp.bfloat16)
    density_out = density_in + cheb_coeffs[0] * cheb_mid.astype(jnp.float32) + cheb_coeffs[1] * cheb_next.astype(jnp.float32)
    return cheb_mid, cheb_next, density_out
```

```python
import functools

import jax
import jax.numpy as jnp
from jax import lax
from jax.experimental import pallas as pl
from jax.experimental.pallas import tpu as pltpu
from jax.sharding import PartitionSpec as P

MESH = pl.DeviceIdType.MESH
OWN, CROSS, PARTNER = 0, 1, 2
ROUNDS = 2
SENDS = 64


def kernel(
    curr_hbm,
    prev_hbm,
    h_hbm,
    listed_hbm,
    counts_hbm,
    mid_ref,
    next_ref,
    first,
    second,
    blocks,
    prev,
    raw,
    total,
    place_rows,
    place,
    listed,
    counts,
    local_sem,
    send_sem,
    first_sem,
    second_sem,
):
    extent_x, extent_y, extent_z = (lax.axis_size(a) for a in ("gx", "gy", "gz"))
    x, y, z = (lax.axis_index(a) for a in ("gx", "gy", "gz"))
    slots, coupled = h_hbm.shape[3], h_hbm.shape[4]
    size = h_hbm.shape[5]
    side = 1 - 2 * (x % 2)
    near_x = (x + side + extent_x) % extent_x
    far_x = (x - side + extent_x) % extent_x
    lean = 1 - 2 * (y % 2)
    other_y = (y + lean + extent_y) % extent_y
    cross_y = (y - lean + extent_y) % extent_y
    up_z = (z + 1) % extent_z
    down_z = (z - 1 + extent_z) % extent_z

    other = (x, other_y, z)
    up, down = (x, y, up_z), (x, y, down_z)
    near, far = (near_x, y, z), (far_x, y, z)
    cross = ((x, cross_y, z), (near_x, cross_y, z), (far_x, cross_y, z))

    inner = (z > 0) & (z < extent_z - 1)
    toward = jnp.where(z < extent_z // 2, 1, -1)

    load_counts = pltpu.make_async_copy(counts_hbm, counts, local_sem.at[0])
    load_listed = pltpu.make_async_copy(listed_hbm, listed, local_sem.at[1])
    load_first = pltpu.make_async_copy(
        curr_hbm.at[0, 0, 0, 0], first.at[0, 0, OWN, 0], local_sem.at[2]
    )
    load_raw = pltpu.make_async_copy(curr_hbm.at[0, 0, 0, 1], raw, local_sem.at[3])
    load_blocks = pltpu.make_async_copy(
        h_hbm.at[0, 0, 0], blocks.at[:, pl.ds(0, coupled)], local_sem.at[4]
    )
    load_prev = pltpu.make_async_copy(prev_hbm.at[0, 0, 0], prev, local_sem.at[5])
    for load in (load_counts, load_listed, load_raw, load_first, load_blocks, load_prev):
        load.start()

    barrier = pltpu.get_barrier_semaphore()
    everyone = (near, far, *cross, up, down, other)
    for device in everyone:
        pl.semaphore_signal(barrier, inc=1, device_id=device, device_id_type=MESH)
    pl.semaphore_wait(barrier, len(everyone))

    pending = []

    def send(step, source, target, semaphore, device, when=None):
        index = len(pending)
        copy = pltpu.make_async_remote_copy(
            src_ref=source,
            dst_ref=target,
            send_sem=send_sem.at[index],
            recv_sem=semaphore,
            device_id=device,
            device_id_type=MESH,
        )
        pending.append((copy, when))
        if when is None:
            copy.start()
        else:
            pl.when(when)(copy.start)

    def arrived(buffer, semaphores, *index):
        ref = buffer.at[index]
        pltpu.make_async_remote_copy(
            src_ref=ref,
            dst_ref=ref,
            send_sem=send_sem.at[0],
            recv_sem=semaphores.at[index],
            device_id=other,
            device_id_type=MESH,
        ).wait_recv()

    def to_other(buffer, semaphores, *index, when=None):
        step, layer, column, group = index
        place_there = (step, layer, PARTNER, group)
        send(
            step,
            buffer.at[index],
            buffer.at[place_there],
            semaphores.at[place_there],
            other,
            when,
        )

    def along_z(step, source, column, group):
        for layer, device in ((1, up), (2, down)):
            at = (step, layer, column, group)
            send(step, source, first.at[at], first_sem.at[at], device)

    def along_xy(buffer, semaphores, step, layer, source, when=None):
        for column, group, device in (
            (OWN, 1, near),
            (OWN, 2, far),
            (CROSS, 1, cross[1]),
            (CROSS, 2, cross[2]),
            (CROSS, 0, cross[0]),
        ):
            at = (step, layer, column, group)
            send(step, source, buffer.at[at], semaphores.at[at], device, when)

    def send_first(step, source):
        along_xy(first, first_sem, step, 0, source)
        along_z(step, source, OWN, 0)
        at = (step, 0, PARTNER, 0)
        send(step, source, first.at[at], first_sem.at[at], other)

    def send_second(step):
        source = second.at[step, 0, OWN, 0]
        at = (step, 1, OWN, 0)
        send(step, source, second.at[at], second_sem.at[at], up, inner)
        send(step, source, second.at[at], second_sem.at[at], down, inner)
        along_xy(second, second_sem, step, 0, source, inner)
        to_other(second, second_sem, step, 0, OWN, 0, when=inner)

    shift_x = (0, side, -side)
    shift_y = (0, -lean, lean)

    def add(buffer, step, layer, column, slot, shift_z, start=False):
        rows = []
        for row in range(slots):
            parts = []
            for group in range(3):
                offset = (shift_x[group] + 1) * 9 + (shift_y[column] + 1) * 3 + shift_z + 1
                parts.append(blocks[row, place[row, offset * slots + slot]])
            rows.append(jnp.concatenate(parts, axis=1))
        product = jnp.dot(
            jnp.concatenate(rows, axis=0),
            buffer[step, layer, column].reshape(3 * size, -1),
            preferred_element_type=jnp.float32,
        )
        if start:
            total[...] = product
        else:
            total[...] += product

    def apply(step, before_blocks):
        arrived(first, first_sem, step, 0, OWN, 1)
        along_z(step, first.at[step, 0, OWN, 1], OWN, 1)
        arrived(second, second_sem, step, 1, OWN, 0)
        along_xy(second, second_sem, step, 1, second.at[step, 1, OWN, 0])
        arrived(first, first_sem, step, 0, OWN, 2)
        along_z(step, first.at[step, 0, OWN, 2], OWN, 2)
        for group in (1, 2, 0):
            arrived(first, first_sem, step, 0, CROSS, group)
            along_z(step, first.at[step, 0, CROSS, group], CROSS, group)
        for group in (1, 2):
            to_other(first, first_sem, step, 0, OWN, group)
        to_other(second, second_sem, step, 1, OWN, 0)

        before_blocks()
        add(first, step, 0, OWN, 0, 0, start=True)
        for layer in (1, 2):
            arrived(first, first_sem, step, layer, OWN, 0)
            to_other(first, first_sem, step, layer, OWN, 0)
        add(first, step, 0, CROSS, 0, 0)

        @pl.when(inner)
        def _():
            for group in (1, 2):
                arrived(second, second_sem, step, 0, OWN, group)

        for group in (1, 2):
            to_other(second, second_sem, step, 0, OWN, group, when=inner)
        for layer in (1, 2):
            arrived(first, first_sem, step, layer, OWN, 1)
            to_other(first, first_sem, step, layer, OWN, 1)

        @pl.when(inner)
        def _():
            for group in (0, 1, 2):
                arrived(second, second_sem, step, 0, CROSS, group)
            add(second, step, 0, OWN, 1, 0)
            add(second, step, 0, CROSS, 1, 0)

        for group in (0, 1, 2):
            arrived(first, first_sem, step, 0, PARTNER, group)
        add(first, step, 0, PARTNER, 0, 0)

        for layer in (1, 2):
            arrived(first, first_sem, step, layer, OWN, 2)
            to_other(first, first_sem, step, layer, OWN, 2)
        for group in (1, 2):
            arrived(second, second_sem, step, 1, OWN, group)
            to_other(second, second_sem, step, 1, OWN, group)

        @pl.when(inner)
        def _():
            for group in (0, 1, 2):
                arrived(second, second_sem, step, 0, PARTNER, group)
            add(second, step, 0, PARTNER, 1, 0)

        add(second, step, 1, OWN, 1, toward)
        for layer in (1, 2):
            shift = -1 if layer == 1 else 1
            add(first, step, layer, OWN, 0, shift)
        for layer in (1, 2):
            shift = -1 if layer == 1 else 1
            for group in (0, 1, 2):
                arrived(first, first_sem, step, layer, CROSS, group)
            add(first, step, layer, CROSS, 0, shift)
            for group in (0, 1, 2):
                arrived(first, first_sem, step, layer, PARTNER, group)
            add(first, step, layer, PARTNER, 0, shift)
        for group in (0, 1, 2):
            arrived(second, second_sem, step, 1, CROSS, group)
        add(second, step, 1, CROSS, 1, toward)
        for group in (0, 1, 2):
            arrived(second, second_sem, step, 1, PARTNER, group)
        add(second, step, 1, PARTNER, 1, toward)

    def settle():
        for copy, when in pending:
            if when is None:
                copy.wait_send()
            else:
                pl.when(when)(copy.wait_send)

    send_first(0, curr_hbm.at[0, 0, 0, 0])
    load_counts.wait()
    load_raw.wait()
    live = counts[0, 0, 0] > 1
    second[0, 0, OWN, 0] = jnp.where(live, raw[...].astype(jnp.float32), 0.0).astype(raw.dtype)
    send_second(0)

    load_listed.wait()
    blocks[:, pl.ds(coupled, 1)] = jnp.zeros((slots, 1, size, size), blocks.dtype)
    lanes = lax.broadcasted_iota(jnp.int32, (1, place_rows.shape[1]), 1)
    for row in range(slots):
        found = jnp.full(lanes.shape, coupled, jnp.int32)
        for item in range(coupled):
            found = jnp.where(lanes == listed[0, 0, 0, row, item], item, found)
        place_rows[pl.ds(row, 1), :] = found
    load_place = pltpu.make_async_copy(place_rows, place, local_sem.at[6])
    load_place.start()
    load_first.wait()
    load_prev.wait()

    def ready():
        load_place.wait()
        load_blocks.wait()

    apply(0, ready)

    def mid_of(row):
        return 2.0 * total[pl.ds(row * size, size), :] - prev[row].astype(jnp.float32)

    mid = mid_of(0).astype(raw.dtype)
    first[1, 0, OWN, 0] = mid
    send_first(1, first.at[1, 0, OWN, 0])
    mid_ref[0, 0, 0, 0] = mid
    mid = jnp.where(live, mid_of(1), 0.0).astype(raw.dtype)
    second[1, 0, OWN, 0] = mid
    send_second(1)
    mid_ref[0, 0, 0, 1] = mid

    apply(1, lambda: None)
    next_ref[0, 0, 0, 0] = (
        2.0 * total[pl.ds(0, size), :] - first[0, 0, OWN, 0].astype(jnp.float32)
    ).astype(raw.dtype)
    next_ref[0, 0, 0, 1] = jnp.where(
        live,
        2.0 * total[pl.ds(size, size), :] - second[0, 0, OWN, 0].astype(jnp.float32),
        0.0,
    ).astype(raw.dtype)
    settle()


def on_device(
    h_blocks, neighbours, block_counts, cheb_prev_in, cheb_curr_in, density_in, cheb_coeffs
):
    slots, coupled, size = h_blocks.shape[3:6]
    field = cheb_curr_in.shape
    probes = field[5]
    kind = cheb_curr_in.dtype
    anywhere = pl.BlockSpec(memory_space=pl.ANY)
    in_vmem = pl.BlockSpec(memory_space=pltpu.VMEM)
    cheb_mid, cheb_next = pl.pallas_call(
        kernel,
        name="two_steps",
        out_shape=(jax.ShapeDtypeStruct(field, kind), jax.ShapeDtypeStruct(field, kind)),
        in_specs=[anywhere] * 5,
        out_specs=(in_vmem, in_vmem),
        scratch_shapes=[
            pltpu.VMEM((ROUNDS, 3, 3, 3, size, probes), kind),
            pltpu.VMEM((ROUNDS, 2, 3, 3, size, probes), kind),
            pltpu.VMEM((slots, coupled + 1, size, size), h_blocks.dtype),
            pltpu.VMEM((slots, size, probes), kind),
            pltpu.VMEM((size, probes), kind),
            pltpu.VMEM((slots * size, probes), jnp.float32),
            pltpu.VMEM((8, 128), jnp.int32),
            pltpu.SMEM((8, 128), jnp.int32),
            pltpu.SMEM(neighbours.shape, jnp.int32),
            pltpu.SMEM(block_counts.shape, jnp.int32),
            pltpu.SemaphoreType.DMA((8,)),
            pltpu.SemaphoreType.DMA((ROUNDS * SENDS,)),
            pltpu.SemaphoreType.DMA((ROUNDS, 3, 3, 3)),
            pltpu.SemaphoreType.DMA((ROUNDS, 2, 3, 3)),
        ],
        compiler_params=pltpu.CompilerParams(
            collective_id=0, has_side_effects=True, vmem_limit_bytes=32 * 2**20
        ),
    )(cheb_curr_in, cheb_prev_in, h_blocks, neighbours, block_counts)
    density_out = (
        density_in
        + cheb_coeffs[0] * cheb_mid.astype(jnp.float32)
        + cheb_coeffs[1] * cheb_next.astype(jnp.float32)
    )
    return (cheb_mid, cheb_next, density_out)


def solution(mesh):
    placed = (
        P("gx", "gy", "gz", None, None, None, None),
        P("gx", "gy", "gz", None, None),
        P("gx", "gy", "gz"),
        P("gx", "gy", "gz", None, None, None),
        P("gx", "gy", "gz", None, None, None),
        P("gx", "gy", "gz", None, None, None),
        P(),
    )
    return jax.shard_map(
        on_device,
        mesh=mesh,
        in_specs=placed,
        out_specs=(
            P("gx", "gy", "gz", None, None, None),
            P("gx", "gy", "gz", None, None, None),
            P("gx", "gy", "gz", None, None, None),
        ),
        check_vma=False,
    )
```

```python
import functools

import jax
import jax.numpy as jnp
from jax import lax
from jax.experimental import pallas as pl
from jax.experimental.pallas import tpu as pltpu
from jax.sharding import PartitionSpec as P

MESH = pl.DeviceIdType.MESH
OWN, CROSS, PARTNER = 0, 1, 2
ROUNDS = 2
SENDS = 64


def kernel(
    curr_hbm,
    prev_hbm,
    h_hbm,
    listed_hbm,
    counts_hbm,
    density_hbm,
    coeffs_hbm,
    mid_ref,
    next_ref,
    density_ref,
    first,
    second,
    blocks,
    prev,
    raw,
    total,
    place_rows,
    place,
    listed,
    counts,
    coeffs,
    local_sem,
    send_sem,
    first_sem,
    second_sem,
):
    extent_x, extent_y, extent_z = (lax.axis_size(a) for a in ("gx", "gy", "gz"))
    x, y, z = (lax.axis_index(a) for a in ("gx", "gy", "gz"))
    slots, coupled = h_hbm.shape[3], h_hbm.shape[4]
    size = h_hbm.shape[5]
    side = 1 - 2 * (x % 2)
    near_x = (x + side + extent_x) % extent_x
    far_x = (x - side + extent_x) % extent_x
    lean = 1 - 2 * (y % 2)
    other_y = (y + lean + extent_y) % extent_y
    cross_y = (y - lean + extent_y) % extent_y
    up_z = (z + 1) % extent_z
    down_z = (z - 1 + extent_z) % extent_z

    other = (x, other_y, z)
    up, down = (x, y, up_z), (x, y, down_z)
    near, far = (near_x, y, z), (far_x, y, z)
    cross = ((x, cross_y, z), (near_x, cross_y, z), (far_x, cross_y, z))

    inner = (z > 0) & (z < extent_z - 1)
    toward = jnp.where(z < extent_z // 2, 1, -1)

    load_counts = pltpu.make_async_copy(counts_hbm, counts, local_sem.at[0])
    load_listed = pltpu.make_async_copy(listed_hbm, listed, local_sem.at[1])
    load_first = pltpu.make_async_copy(
        curr_hbm.at[0, 0, 0, 0], first.at[0, 0, OWN, 0], local_sem.at[2]
    )
    load_raw = pltpu.make_async_copy(curr_hbm.at[0, 0, 0, 1], raw, local_sem.at[3])
    load_blocks = pltpu.make_async_copy(
        h_hbm.at[0, 0, 0], blocks.at[:, pl.ds(0, coupled)], local_sem.at[4]
    )
    load_prev = pltpu.make_async_copy(prev_hbm.at[0, 0, 0], prev, local_sem.at[5])
    load_density = pltpu.make_async_copy(density_hbm, density_ref, local_sem.at[7])
    load_coeffs = pltpu.make_async_copy(coeffs_hbm, coeffs, local_sem.at[8])
    for load in (
        load_counts,
        load_listed,
        load_raw,
        load_first,
        load_blocks,
        load_prev,
        load_density,
        load_coeffs,
    ):
        load.start()

    barrier = pltpu.get_barrier_semaphore()
    everyone = (near, far, *cross, up, down, other)
    for device in everyone:
        pl.semaphore_signal(barrier, inc=1, device_id=device, device_id_type=MESH)
    pl.semaphore_wait(barrier, len(everyone))

    pending = []

    def send(step, source, target, semaphore, device, when=None):
        index = len(pending)
        copy = pltpu.make_async_remote_copy(
            src_ref=source,
            dst_ref=target,
            send_sem=send_sem.at[index],
            recv_sem=semaphore,
            device_id=device,
            device_id_type=MESH,
        )
        pending.append((copy, when))
        if when is None:
            copy.start()
        else:
            pl.when(when)(copy.start)

    def arrived(buffer, semaphores, *index):
        ref = buffer.at[index]
        pltpu.make_async_remote_copy(
            src_ref=ref,
            dst_ref=ref,
            send_sem=send_sem.at[0],
            recv_sem=semaphores.at[index],
            device_id=other,
            device_id_type=MESH,
        ).wait_recv()

    def to_other(buffer, semaphores, *index, when=None):
        step, layer, column, group = index
        place_there = (step, layer, PARTNER, group)
        send(
            step,
            buffer.at[index],
            buffer.at[place_there],
            semaphores.at[place_there],
            other,
            when,
        )

    def along_z(step, source, column, group):
        for layer, device in ((1, up), (2, down)):
            at = (step, layer, column, group)
            send(step, source, first.at[at], first_sem.at[at], device)

    def along_xy(buffer, semaphores, step, layer, source, when=None):
        for column, group, device in (
            (OWN, 1, near),
            (OWN, 2, far),
            (CROSS, 1, cross[1]),
            (CROSS, 2, cross[2]),
            (CROSS, 0, cross[0]),
        ):
            at = (step, layer, column, group)
            send(step, source, buffer.at[at], semaphores.at[at], device, when)

    def send_first(step, source):
        along_xy(first, first_sem, step, 0, source)
        along_z(step, source, OWN, 0)
        at = (step, 0, PARTNER, 0)
        send(step, source, first.at[at], first_sem.at[at], other)

    def send_second(step):
        source = second.at[step, 0, OWN, 0]
        at = (step, 1, OWN, 0)
        send(step, source, second.at[at], second_sem.at[at], up, inner)
        send(step, source, second.at[at], second_sem.at[at], down, inner)
        along_xy(second, second_sem, step, 0, source, inner)
        to_other(second, second_sem, step, 0, OWN, 0, when=inner)

    shift_x = (0, side, -side)
    shift_y = (0, -lean, lean)

    def add(buffer, step, layer, column, slot, shift_z, start=False):
        rows = []
        for row in range(slots):
            parts = []
            for group in range(3):
                offset = (shift_x[group] + 1) * 9 + (shift_y[column] + 1) * 3 + shift_z + 1
                parts.append(blocks[row, place[row, offset * slots + slot]])
            rows.append(jnp.concatenate(parts, axis=1))
        product = jnp.dot(
            jnp.concatenate(rows, axis=0),
            buffer[step, layer, column].reshape(3 * size, -1),
            preferred_element_type=jnp.float32,
        )
        if start:
            total[...] = product
        else:
            total[...] += product

    def apply(step, before_blocks):
        arrived(first, first_sem, step, 0, OWN, 1)
        along_z(step, first.at[step, 0, OWN, 1], OWN, 1)
        arrived(second, second_sem, step, 1, OWN, 0)
        along_xy(second, second_sem, step, 1, second.at[step, 1, OWN, 0])
        arrived(first, first_sem, step, 0, OWN, 2)
        along_z(step, first.at[step, 0, OWN, 2], OWN, 2)
        for group in (1, 2, 0):
            arrived(first, first_sem, step, 0, CROSS, group)
            along_z(step, first.at[step, 0, CROSS, group], CROSS, group)
        for group in (1, 2):
            to_other(first, first_sem, step, 0, OWN, group)
        to_other(second, second_sem, step, 1, OWN, 0)

        before_blocks()
        add(first, step, 0, OWN, 0, 0, start=True)
        for layer in (1, 2):
            arrived(first, first_sem, step, layer, OWN, 0)
            to_other(first, first_sem, step, layer, OWN, 0)
        add(first, step, 0, CROSS, 0, 0)

        @pl.when(inner)
        def _():
            for group in (1, 2):
                arrived(second, second_sem, step, 0, OWN, group)

        for group in (1, 2):
            to_other(second, second_sem, step, 0, OWN, group, when=inner)
        for layer in (1, 2):
            arrived(first, first_sem, step, layer, OWN, 1)
            to_other(first, first_sem, step, layer, OWN, 1)

        @pl.when(inner)
        def _():
            for group in (0, 1, 2):
                arrived(second, second_sem, step, 0, CROSS, group)
            add(second, step, 0, OWN, 1, 0)
            add(second, step, 0, CROSS, 1, 0)

        for group in (0, 1, 2):
            arrived(first, first_sem, step, 0, PARTNER, group)
        add(first, step, 0, PARTNER, 0, 0)

        for layer in (1, 2):
            arrived(first, first_sem, step, layer, OWN, 2)
            to_other(first, first_sem, step, layer, OWN, 2)
        for group in (1, 2):
            arrived(second, second_sem, step, 1, OWN, group)
            to_other(second, second_sem, step, 1, OWN, group)

        @pl.when(inner)
        def _():
            for group in (0, 1, 2):
                arrived(second, second_sem, step, 0, PARTNER, group)
            add(second, step, 0, PARTNER, 1, 0)

        add(second, step, 1, OWN, 1, toward)
        for layer in (1, 2):
            shift = -1 if layer == 1 else 1
            add(first, step, layer, OWN, 0, shift)
        for layer in (1, 2):
            shift = -1 if layer == 1 else 1
            for group in (0, 1, 2):
                arrived(first, first_sem, step, layer, CROSS, group)
            add(first, step, layer, CROSS, 0, shift)
            for group in (0, 1, 2):
                arrived(first, first_sem, step, layer, PARTNER, group)
            add(first, step, layer, PARTNER, 0, shift)
        for group in (0, 1, 2):
            arrived(second, second_sem, step, 1, CROSS, group)
        add(second, step, 1, CROSS, 1, toward)
        for group in (0, 1, 2):
            arrived(second, second_sem, step, 1, PARTNER, group)
        add(second, step, 1, PARTNER, 1, toward)

    def settle():
        for copy, when in pending:
            if when is None:
                copy.wait_send()
            else:
                pl.when(when)(copy.wait_send)

    send_first(0, curr_hbm.at[0, 0, 0, 0])
    load_counts.wait()
    load_raw.wait()
    live = counts[0, 0, 0] > 1
    second[0, 0, OWN, 0] = jnp.where(live, raw[...].astype(jnp.float32), 0.0).astype(raw.dtype)
    send_second(0)

    load_listed.wait()
    blocks[:, pl.ds(coupled, 1)] = jnp.zeros((slots, 1, size, size), blocks.dtype)
    lanes = lax.broadcasted_iota(jnp.int32, (1, place_rows.shape[1]), 1)
    for row in range(slots):
        found = jnp.full(lanes.shape, coupled, jnp.int32)
        for item in range(coupled):
            found = jnp.where(lanes == listed[0, 0, 0, row, item], item, found)
        place_rows[pl.ds(row, 1), :] = found
    load_place = pltpu.make_async_copy(place_rows, place, local_sem.at[6])
    load_place.start()
    load_first.wait()
    load_prev.wait()

    def ready():
        load_place.wait()
        load_blocks.wait()

    apply(0, ready)

    def mid_of(row):
        return 2.0 * total[pl.ds(row * size, size), :] - prev[row].astype(jnp.float32)

    mid = mid_of(0).astype(raw.dtype)
    first[1, 0, OWN, 0] = mid
    send_first(1, first.at[1, 0, OWN, 0])
    mid_ref[0, 0, 0, 0] = mid
    mid = jnp.where(live, mid_of(1), 0.0).astype(raw.dtype)
    second[1, 0, OWN, 0] = mid
    send_second(1)
    mid_ref[0, 0, 0, 1] = mid

    load_density.wait()
    load_coeffs.wait()
    density_ref[...] += coeffs[0] * mid_ref[...].astype(jnp.float32)
    apply(1, lambda: None)
    for row, held in ((0, first), (1, second)):
        value = 2.0 * total[pl.ds(row * size, size), :] - held[0, 0, OWN, 0].astype(jnp.float32)
        if row:
            value = jnp.where(live, value, 0.0)
        value = value.astype(raw.dtype)
        next_ref[0, 0, 0, row] = value
        density_ref[0, 0, 0, row] += coeffs[1] * value.astype(jnp.float32)
    settle()


def hand_over(*refs):
    count = len(refs) // 2
    sources, targets, semaphores = refs[:count], refs[count : 2 * count], refs[-1]
    copies = [
        pltpu.make_async_copy(source, target, semaphores.at[index])
        for index, (source, target) in enumerate(zip(sources, targets))
    ]
    for copy in copies:
        copy.start()
    for copy in copies:
        copy.wait()


def on_device(
    h_blocks, neighbours, block_counts, cheb_prev_in, cheb_curr_in, density_in, cheb_coeffs
):
    slots, coupled, size = h_blocks.shape[3:6]
    field = cheb_curr_in.shape
    probes = field[5]
    kind = cheb_curr_in.dtype
    in_hbm = pl.BlockSpec(memory_space=pltpu.HBM)
    kept = functools.partial(pltpu.with_memory_space_constraint, memory_space=pltpu.HBM)
    in_vmem = pl.BlockSpec(memory_space=pltpu.VMEM)
    results = (
        jax.ShapeDtypeStruct(field, kind),
        jax.ShapeDtypeStruct(field, kind),
        jax.ShapeDtypeStruct(field, jnp.float32),
    )
    made = pl.pallas_call(
        kernel,
        name="two_steps",
        out_shape=results,
        in_specs=[in_hbm] * 7,
        out_specs=(in_vmem,) * 3,
        scratch_shapes=[
            pltpu.VMEM((ROUNDS, 3, 3, 3, size, probes), kind),
            pltpu.VMEM((ROUNDS, 2, 3, 3, size, probes), kind),
            pltpu.VMEM((slots, coupled + 1, size, size), h_blocks.dtype),
            pltpu.VMEM((slots, size, probes), kind),
            pltpu.VMEM((size, probes), kind),
            pltpu.VMEM((slots * size, probes), jnp.float32),
            pltpu.VMEM((8, 128), jnp.int32),
            pltpu.SMEM((8, 128), jnp.int32),
            pltpu.SMEM(neighbours.shape, jnp.int32),
            pltpu.SMEM(block_counts.shape, jnp.int32),
            pltpu.SMEM(cheb_coeffs.shape, jnp.float32),
            pltpu.SemaphoreType.DMA((9,)),
            pltpu.SemaphoreType.DMA((ROUNDS * SENDS,)),
            pltpu.SemaphoreType.DMA((ROUNDS, 3, 3, 3)),
            pltpu.SemaphoreType.DMA((ROUNDS, 2, 3, 3)),
        ],
        compiler_params=pltpu.CompilerParams(
            collective_id=0, has_side_effects=True, vmem_limit_bytes=32 * 2**20
        ),
    )(
        kept(cheb_curr_in),
        kept(cheb_prev_in),
        kept(h_blocks),
        kept(neighbours),
        block_counts,
        kept(density_in),
        kept(cheb_coeffs),
    )
    return tuple(
        pl.pallas_call(
            hand_over,
            name="hand_over",
            out_shape=results,
            in_specs=[pl.BlockSpec(memory_space=pl.ANY)] * 3,
            out_specs=(in_hbm,) * 3,
            scratch_shapes=[pltpu.SemaphoreType.DMA((3,))],
        )(*made)
    )


def solution(mesh):
    placed = (
        P("gx", "gy", "gz", None, None, None, None),
        P("gx", "gy", "gz", None, None),
        P("gx", "gy", "gz"),
        P("gx", "gy", "gz", None, None, None),
        P("gx", "gy", "gz", None, None, None),
        P("gx", "gy", "gz", None, None, None),
        P(),
    )
    return jax.shard_map(
        on_device,
        mesh=mesh,
        in_specs=placed,
        out_specs=(
            P("gx", "gy", "gz", None, None, None),
            P("gx", "gy", "gz", None, None, None),
            P("gx", "gy", "gz", None, None, None),
        ),
        check_vma=False,
    )
```

```python
import functools

import jax
import jax.numpy as jnp
from jax import lax
from jax.experimental import pallas as pl
from jax.experimental.pallas import tpu as pltpu
from jax.sharding import PartitionSpec as P

MESH = pl.DeviceIdType.MESH
OWN, CROSS, PARTNER = 0, 1, 2
ROUNDS = 2
SENDS = 64


def kernel(
    curr_hbm,
    prev_hbm,
    h_hbm,
    listed_hbm,
    counts_hbm,
    density_hbm,
    coeffs_hbm,
    mid_ref,
    next_ref,
    density_ref,
    first,
    second,
    blocks,
    prev,
    raw,
    total,
    place_rows,
    place,
    listed,
    counts,
    coeffs,
    local_sem,
    send_sem,
    first_sem,
    second_sem,
):
    extent_x, extent_y, extent_z = (lax.axis_size(a) for a in ("gx", "gy", "gz"))
    x, y, z = (lax.axis_index(a) for a in ("gx", "gy", "gz"))
    slots, coupled = h_hbm.shape[3], h_hbm.shape[4]
    size = h_hbm.shape[5]
    side = 1 - 2 * (x % 2)
    near_x = (x + side + extent_x) % extent_x
    far_x = (x - side + extent_x) % extent_x
    lean = 1 - 2 * (y % 2)
    other_y = (y + lean + extent_y) % extent_y
    cross_y = (y - lean + extent_y) % extent_y
    up_z = (z + 1) % extent_z
    down_z = (z - 1 + extent_z) % extent_z

    other = (x, other_y, z)
    up, down = (x, y, up_z), (x, y, down_z)
    near, far = (near_x, y, z), (far_x, y, z)
    cross = ((x, cross_y, z), (near_x, cross_y, z), (far_x, cross_y, z))

    inner = (z > 0) & (z < extent_z - 1)
    toward = jnp.where(z < extent_z // 2, 1, -1)

    load_counts = pltpu.make_async_copy(counts_hbm, counts, local_sem.at[0])
    load_listed = pltpu.make_async_copy(listed_hbm, listed, local_sem.at[1])
    load_first = pltpu.make_async_copy(
        curr_hbm.at[0, 0, 0, 0], first.at[0, 0, OWN, 0], local_sem.at[2]
    )
    load_raw = pltpu.make_async_copy(curr_hbm.at[0, 0, 0, 1], raw, local_sem.at[3])
    load_blocks = pltpu.make_async_copy(
        h_hbm.at[0, 0, 0], blocks.at[:, pl.ds(0, coupled)], local_sem.at[4]
    )
    load_prev = pltpu.make_async_copy(prev_hbm.at[0, 0, 0], prev, local_sem.at[5])
    load_density = pltpu.make_async_copy(density_hbm, density_ref, local_sem.at[7])
    load_coeffs = pltpu.make_async_copy(coeffs_hbm, coeffs, local_sem.at[8])
    for load in (
        load_counts,
        load_listed,
        load_raw,
        load_first,
        load_blocks,
        load_prev,
        load_density,
        load_coeffs,
    ):
        load.start()

    barrier = pltpu.get_barrier_semaphore()
    everyone = (near, far, *cross, up, down, other)
    for device in everyone:
        pl.semaphore_signal(barrier, inc=1, device_id=device, device_id_type=MESH)
    pl.semaphore_wait(barrier, len(everyone))

    pending = []

    def send(step, source, target, semaphore, device, when=None):
        index = len(pending)
        copy = pltpu.make_async_remote_copy(
            src_ref=source,
            dst_ref=target,
            send_sem=send_sem.at[index],
            recv_sem=semaphore,
            device_id=device,
            device_id_type=MESH,
        )
        pending.append((copy, when))
        if when is None:
            copy.start()
        else:
            pl.when(when)(copy.start)

    def arrived(buffer, semaphores, *index):
        ref = buffer.at[index]
        pltpu.make_async_remote_copy(
            src_ref=ref,
            dst_ref=ref,
            send_sem=send_sem.at[0],
            recv_sem=semaphores.at[index],
            device_id=other,
            device_id_type=MESH,
        ).wait_recv()

    def to_other(buffer, semaphores, *index, when=None):
        step, layer, column, group = index
        place_there = (step, layer, PARTNER, group)
        send(
            step,
            buffer.at[index],
            buffer.at[place_there],
            semaphores.at[place_there],
            other,
            when,
        )

    def along_z(step, source, column, group):
        for layer, device in ((1, up), (2, down)):
            at = (step, layer, column, group)
            send(step, source, first.at[at], first_sem.at[at], device)

    def along_xy(buffer, semaphores, step, layer, source, when=None):
        for column, group, device in (
            (OWN, 1, near),
            (OWN, 2, far),
            (CROSS, 1, cross[1]),
            (CROSS, 2, cross[2]),
            (CROSS, 0, cross[0]),
        ):
            at = (step, layer, column, group)
            send(step, source, buffer.at[at], semaphores.at[at], device, when)

    def send_first(step, source):
        along_xy(first, first_sem, step, 0, source)
        along_z(step, source, OWN, 0)
        at = (step, 0, PARTNER, 0)
        send(step, source, first.at[at], first_sem.at[at], other)

    def send_second(step):
        source = second.at[step, 0, OWN, 0]
        at = (step, 1, OWN, 0)
        send(step, source, second.at[at], second_sem.at[at], up, inner)
        send(step, source, second.at[at], second_sem.at[at], down, inner)
        along_xy(second, second_sem, step, 0, source, inner)
        to_other(second, second_sem, step, 0, OWN, 0, when=inner)

    shift_x = (0, side, -side)
    shift_y = (0, -lean, lean)

    def add(buffer, step, layer, column, slot, shift_z, start=False):
        rows = []
        for row in range(slots):
            parts = []
            for group in range(3):
                offset = (shift_x[group] + 1) * 9 + (shift_y[column] + 1) * 3 + shift_z + 1
                parts.append(blocks[row, place[row, offset * slots + slot]])
            rows.append(jnp.concatenate(parts, axis=1))
        product = jnp.dot(
            jnp.concatenate(rows, axis=0),
            buffer[step, layer, column].reshape(3 * size, -1),
            preferred_element_type=jnp.float32,
        )
        if start:
            total[...] = product
        else:
            total[...] += product

    def apply(step, before_blocks):
        arrived(first, first_sem, step, 0, OWN, 1)
        along_z(step, first.at[step, 0, OWN, 1], OWN, 1)
        arrived(second, second_sem, step, 1, OWN, 0)
        along_xy(second, second_sem, step, 1, second.at[step, 1, OWN, 0])
        arrived(first, first_sem, step, 0, OWN, 2)
        along_z(step, first.at[step, 0, OWN, 2], OWN, 2)
        for group in (1, 2, 0):
            arrived(first, first_sem, step, 0, CROSS, group)
            along_z(step, first.at[step, 0, CROSS, group], CROSS, group)
        for group in (1, 2):
            to_other(first, first_sem, step, 0, OWN, group)
        to_other(second, second_sem, step, 1, OWN, 0)

        before_blocks()
        add(first, step, 0, OWN, 0, 0, start=True)
        for layer in (1, 2):
            arrived(first, first_sem, step, layer, OWN, 0)
            to_other(first, first_sem, step, layer, OWN, 0)
        add(first, step, 0, CROSS, 0, 0)

        @pl.when(inner)
        def _():
            for group in (1, 2):
                arrived(second, second_sem, step, 0, OWN, group)

        for group in (1, 2):
            to_other(second, second_sem, step, 0, OWN, group, when=inner)
        for layer in (1, 2):
            arrived(first, first_sem, step, layer, OWN, 1)
            to_other(first, first_sem, step, layer, OWN, 1)

        @pl.when(inner)
        def _():
            for group in (0, 1, 2):
                arrived(second, second_sem, step, 0, CROSS, group)
            add(second, step, 0, OWN, 1, 0)
            add(second, step, 0, CROSS, 1, 0)

        for group in (0, 1, 2):
            arrived(first, first_sem, step, 0, PARTNER, group)
        add(first, step, 0, PARTNER, 0, 0)

        for layer in (1, 2):
            arrived(first, first_sem, step, layer, OWN, 2)
            to_other(first, first_sem, step, layer, OWN, 2)
        for group in (1, 2):
            arrived(second, second_sem, step, 1, OWN, group)
            to_other(second, second_sem, step, 1, OWN, group)

        @pl.when(inner)
        def _():
            for group in (0, 1, 2):
                arrived(second, second_sem, step, 0, PARTNER, group)
            add(second, step, 0, PARTNER, 1, 0)

        add(second, step, 1, OWN, 1, toward)
        for layer in (1, 2):
            shift = -1 if layer == 1 else 1
            add(first, step, layer, OWN, 0, shift)
        for layer in (1, 2):
            shift = -1 if layer == 1 else 1
            for group in (0, 1, 2):
                arrived(first, first_sem, step, layer, CROSS, group)
            add(first, step, layer, CROSS, 0, shift)
            for group in (0, 1, 2):
                arrived(first, first_sem, step, layer, PARTNER, group)
            add(first, step, layer, PARTNER, 0, shift)
        for group in (0, 1, 2):
            arrived(second, second_sem, step, 1, CROSS, group)
        add(second, step, 1, CROSS, 1, toward)
        for group in (0, 1, 2):
            arrived(second, second_sem, step, 1, PARTNER, group)
        add(second, step, 1, PARTNER, 1, toward)

    def settle():
        for copy, when in pending:
            if when is None:
                copy.wait_send()
            else:
                pl.when(when)(copy.wait_send)

    send_first(0, curr_hbm.at[0, 0, 0, 0])
    load_counts.wait()
    load_raw.wait()
    live = counts[0, 0, 0] > 1
    second[0, 0, OWN, 0] = jnp.where(live, raw[...].astype(jnp.float32), 0.0).astype(raw.dtype)
    send_second(0)

    load_listed.wait()
    blocks[:, pl.ds(coupled, 1)] = jnp.zeros((slots, 1, size, size), blocks.dtype)
    lanes = lax.broadcasted_iota(jnp.int32, (1, place_rows.shape[1]), 1)
    for row in range(slots):
        found = jnp.full(lanes.shape, coupled, jnp.int32)
        for item in range(coupled):
            found = jnp.where(lanes == listed[0, 0, 0, row, item], item, found)
        place_rows[pl.ds(row, 1), :] = found
    load_place = pltpu.make_async_copy(place_rows, place, local_sem.at[6])
    load_place.start()
    load_first.wait()
    load_prev.wait()

    def ready():
        load_place.wait()
        load_blocks.wait()

    apply(0, ready)

    def mid_of(row):
        return 2.0 * total[pl.ds(row * size, size), :] - prev[row].astype(jnp.float32)

    mid = mid_of(0).astype(raw.dtype)
    first[1, 0, OWN, 0] = mid
    send_first(1, first.at[1, 0, OWN, 0])
    mid_ref[0, 0, 0, 0] = mid
    mid = jnp.where(live, mid_of(1), 0.0).astype(raw.dtype)
    second[1, 0, OWN, 0] = mid
    send_second(1)
    mid_ref[0, 0, 0, 1] = mid

    load_density.wait()
    load_coeffs.wait()
    density_ref[...] += coeffs[0] * mid_ref[...].astype(jnp.float32)
    apply(1, lambda: None)
    for row, held in ((0, first), (1, second)):
        value = 2.0 * total[pl.ds(row * size, size), :] - held[0, 0, OWN, 0].astype(jnp.float32)
        if row:
            value = jnp.where(live, value, 0.0)
        value = value.astype(raw.dtype)
        next_ref[0, 0, 0, row] = value
        density_ref[0, 0, 0, row] += coeffs[1] * value.astype(jnp.float32)
    settle()


def hand_over(*refs):
    count = len(refs) // 2
    sources, targets, semaphores = refs[:count], refs[count : 2 * count], refs[-1]
    copies = [
        pltpu.make_async_copy(source, target, semaphores.at[index])
        for index, (source, target) in enumerate(zip(sources, targets))
    ]
    for copy in copies:
        copy.start()
    for copy in copies:
        copy.wait()


def on_device(
    h_blocks, neighbours, block_counts, cheb_prev_in, cheb_curr_in, density_in, cheb_coeffs
):
    slots, coupled, size = h_blocks.shape[3:6]
    field = cheb_curr_in.shape
    probes = field[5]
    kind = cheb_curr_in.dtype
    in_hbm = pl.BlockSpec(memory_space=pltpu.HBM)
    kept = functools.partial(pltpu.with_memory_space_constraint, memory_space=pltpu.HBM)
    in_vmem = pl.BlockSpec(memory_space=pltpu.VMEM)
    results = (
        jax.ShapeDtypeStruct(field, kind),
        jax.ShapeDtypeStruct(field, kind),
        jax.ShapeDtypeStruct(field, jnp.float32),
    )
    made = pl.pallas_call(
        kernel,
        name="two_steps",
        out_shape=results,
        in_specs=[in_hbm] * 7,
        out_specs=(in_vmem,) * 3,
        scratch_shapes=[
            pltpu.VMEM((ROUNDS, 3, 3, 3, size, probes), kind),
            pltpu.VMEM((ROUNDS, 2, 3, 3, size, probes), kind),
            pltpu.VMEM((slots, coupled + 1, size, size), h_blocks.dtype),
            pltpu.VMEM((slots, size, probes), kind),
            pltpu.VMEM((size, probes), kind),
            pltpu.VMEM((slots * size, probes), jnp.float32),
            pltpu.VMEM((8, 128), jnp.int32),
            pltpu.SMEM((8, 128), jnp.int32),
            pltpu.SMEM(neighbours.shape, jnp.int32),
            pltpu.SMEM(block_counts.shape, jnp.int32),
            pltpu.SMEM(cheb_coeffs.shape, jnp.float32),
            pltpu.SemaphoreType.DMA((9,)),
            pltpu.SemaphoreType.DMA((ROUNDS * SENDS,)),
            pltpu.SemaphoreType.DMA((ROUNDS, 3, 3, 3)),
            pltpu.SemaphoreType.DMA((ROUNDS, 2, 3, 3)),
        ],
        compiler_params=pltpu.CompilerParams(
            collective_id=0, has_side_effects=True, vmem_limit_bytes=32 * 2**20
        ),
    )(
        kept(cheb_curr_in),
        kept(cheb_prev_in),
        kept(h_blocks),
        kept(neighbours),
        block_counts,
        kept(density_in),
        kept(cheb_coeffs),
    )
    return tuple(
        pl.pallas_call(
            hand_over,
            name="hand_over",
            out_shape=results,
            in_specs=[in_vmem] * 3,
            out_specs=(in_hbm,) * 3,
            scratch_shapes=[pltpu.SemaphoreType.DMA((3,))],
        )(*(pltpu.with_memory_space_constraint(array, pltpu.VMEM) for array in made))
    )


def solution(mesh):
    placed = (
        P("gx", "gy", "gz", None, None, None, None),
        P("gx", "gy", "gz", None, None),
        P("gx", "gy", "gz"),
        P("gx", "gy", "gz", None, None, None),
        P("gx", "gy", "gz", None, None, None),
        P("gx", "gy", "gz", None, None, None),
        P(),
    )
    return jax.shard_map(
        on_device,
        mesh=mesh,
        in_specs=placed,
        out_specs=(
            P("gx", "gy", "gz", None, None, None),
            P("gx", "gy", "gz", None, None, None),
            P("gx", "gy", "gz", None, None, None),
        ),
        check_vma=False,
    )
```

```python
import functools

import jax
import jax.numpy as jnp
from jax import lax
from jax.experimental import pallas as pl
from jax.experimental.pallas import tpu as pltpu
from jax.sharding import PartitionSpec as P

MESH = pl.DeviceIdType.MESH
ROUNDS = 2

OWN, CROSS, PARTNER = 0, 1, 2
STAY, NEAR, FAR, AHEAD, BEHIND = 0, 1, 2, 3, 4
UP, DOWN, BOTH = 1, 2, 3
WAIT, SEND, ADD = 0, 1, 2

FIRST_SENDS = (
    ((0, 0, 0, 2), FAR, OWN, STAY),
    ((0, 0, 0, 1), NEAR, OWN, STAY),
    ((0, 0, 1, 2), FAR, CROSS, STAY),
    ((0, 0, 1, 1), NEAR, CROSS, STAY),
    ((0, 0, 1, 0), STAY, CROSS, STAY),
    ((0, 1, 0, 0), STAY, OWN, UP),
    ((0, 2, 0, 0), STAY, OWN, DOWN),
    ((0, 0, 2, 0), STAY, PARTNER, STAY),
)
SECOND_SENDS = (
    ((1, 1, 0, 0), STAY, OWN, BOTH),
    ((1, 0, 1, 1), NEAR, CROSS, STAY),
    ((1, 0, 0, 2), FAR, OWN, STAY),
    ((1, 0, 0, 1), NEAR, OWN, STAY),
    ((1, 0, 1, 0), STAY, CROSS, STAY),
    ((1, 0, 2, 0), STAY, PARTNER, STAY),
)
ORDER = (
    (WAIT, (0, 0, 2, 0)),
    (WAIT, (1, 0, 2, 0)),
    (WAIT, (0, 1, 0, 0)),
    (WAIT, (0, 2, 0, 0)),
    (
        SEND,
        (0, 1, 0, 0),
        (
            ((0, 1, 2, 0), STAY, PARTNER, STAY),
        ),
    ),
    (
        SEND,
        (0, 2, 0, 0),
        (
            ((0, 2, 2, 0), STAY, PARTNER, STAY),
        ),
    ),
    (WAIT, (0, 0, 1, 0)),
    (
        SEND,
        (0, 0, 1, 0),
        (
            ((0, 1, 1, 0), STAY, OWN, UP),
            ((0, 2, 1, 0), STAY, OWN, DOWN),
        ),
    ),
    (WAIT, (1, 1, 0, 0)),
    (
        SEND,
        (1, 1, 0, 0),
        (
            ((1, 1, 0, 2), FAR, OWN, STAY),
            ((1, 1, 0, 1), NEAR, OWN, STAY),
            ((1, 1, 1, 2), FAR, CROSS, STAY),
            ((1, 1, 1, 1), NEAR, CROSS, STAY),
            ((1, 1, 1, 0), STAY, CROSS, STAY),
            ((1, 1, 2, 0), STAY, PARTNER, STAY),
        ),
    ),
    (WAIT, (0, 1, 2, 0)),
    (WAIT, (0, 2, 2, 0)),
    (WAIT, (0, 0, 0, 2)),
    (
        SEND,
        (0, 0, 0, 2),
        (
            ((0, 1, 0, 2), STAY, OWN, UP),
            ((0, 2, 0, 2), STAY, OWN, DOWN),
            ((0, 0, 2, 2), STAY, PARTNER, STAY),
        ),
    ),
    (WAIT, (0, 0, 0, 1)),
    (
        SEND,
        (0, 0, 0, 1),
        (
            ((0, 1, 0, 1), STAY, OWN, UP),
            ((0, 2, 0, 1), STAY, OWN, DOWN),
            ((0, 0, 2, 1), STAY, PARTNER, STAY),
        ),
    ),
    (WAIT, (0, 0, 1, 1)),
    (
        SEND,
        (0, 0, 1, 1),
        (
            ((0, 1, 1, 1), STAY, OWN, UP),
            ((0, 2, 1, 1), STAY, OWN, DOWN),
        ),
    ),
    (WAIT, (1, 1, 2, 0)),
    (WAIT, (0, 0, 1, 2)),
    (
        SEND,
        (0, 0, 1, 2),
        (
            ((0, 1, 1, 2), STAY, OWN, UP),
            ((0, 2, 1, 2), STAY, OWN, DOWN),
        ),
    ),
    (ADD, (0, 0, 0)),
    (WAIT, (1, 0, 1, 1)),
    (
        SEND,
        (1, 0, 1, 1),
        (
            ((1, 0, 1, 2), AHEAD, OWN, STAY),
        ),
    ),
    (WAIT, (0, 0, 2, 2)),
    (ADD, (0, 0, 1)),
    (WAIT, (0, 0, 2, 1)),
    (WAIT, (1, 0, 1, 0)),
    (ADD, (0, 0, 2)),
    (WAIT, (0, 1, 1, 0)),
    (WAIT, (0, 2, 1, 0)),
    (WAIT, (1, 0, 0, 2)),
    (
        SEND,
        (1, 0, 0, 2),
        (
            ((1, 0, 2, 2), STAY, PARTNER, STAY),
        ),
    ),
    (WAIT, (1, 0, 0, 1)),
    (
        SEND,
        (1, 0, 0, 1),
        (
            ((1, 0, 2, 1), STAY, PARTNER, STAY),
        ),
    ),
    (WAIT, (1, 1, 1, 0)),
    (WAIT, (0, 1, 0, 2)),
    (WAIT, (0, 2, 0, 2)),
    (
        SEND,
        (0, 1, 0, 2),
        (
            ((0, 1, 2, 2), STAY, PARTNER, STAY),
        ),
    ),
    (
        SEND,
        (0, 2, 0, 2),
        (
            ((0, 2, 2, 2), STAY, PARTNER, STAY),
        ),
    ),
    (ADD, (1, 0, 0)),
    (WAIT, (1, 0, 2, 2)),
    (WAIT, (1, 0, 2, 1)),
    (WAIT, (0, 1, 0, 1)),
    (WAIT, (0, 2, 0, 1)),
    (
        SEND,
        (0, 1, 0, 1),
        (
            ((0, 1, 2, 1), STAY, PARTNER, STAY),
        ),
    ),
    (
        SEND,
        (0, 2, 0, 1),
        (
            ((0, 2, 2, 1), STAY, PARTNER, STAY),
        ),
    ),
    (WAIT, (1, 1, 0, 2)),
    (
        SEND,
        (1, 1, 0, 2),
        (
            ((1, 1, 2, 2), STAY, PARTNER, STAY),
        ),
    ),
    (WAIT, (1, 1, 0, 1)),
    (WAIT, (1, 0, 1, 2)),
    (
        SEND,
        (1, 1, 0, 1),
        (
            ((1, 1, 2, 1), STAY, PARTNER, STAY),
        ),
    ),
    (WAIT, (1, 1, 1, 1)),
    (WAIT, (0, 1, 2, 2)),
    (WAIT, (0, 2, 2, 2)),
    (ADD, (1, 0, 2)),
    (ADD, (0, 1, 0)),
    (ADD, (0, 2, 0)),
    (WAIT, (1, 1, 1, 2)),
    (ADD, (1, 1, 0)),
    (ADD, (1, 0, 1)),
    (WAIT, (0, 1, 2, 1)),
    (WAIT, (0, 2, 2, 1)),
    (WAIT, (1, 1, 2, 2)),
    (WAIT, (0, 1, 1, 1)),
    (WAIT, (0, 2, 1, 1)),
    (ADD, (1, 1, 1)),
    (WAIT, (1, 1, 2, 1)),
    (WAIT, (0, 1, 1, 2)),
    (WAIT, (0, 2, 1, 2)),
    (ADD, (0, 1, 2)),
    (ADD, (0, 2, 2)),
    (ADD, (1, 1, 2)),
    (ADD, (0, 1, 1)),
    (ADD, (0, 2, 1)),
)


def kernel(
    curr_hbm,
    prev_hbm,
    h_hbm,
    listed_hbm,
    counts_hbm,
    density_hbm,
    coeffs_hbm,
    mid_ref,
    next_ref,
    density_ref,
    first,
    second,
    blocks,
    prev,
    raw,
    total,
    place_rows,
    place,
    listed,
    counts,
    coeffs,
    local_sem,
    send_sem,
    first_sem,
    second_sem,
):
    extent_x, extent_y, extent_z = (lax.axis_size(a) for a in ("gx", "gy", "gz"))
    x, y, z = (lax.axis_index(a) for a in ("gx", "gy", "gz"))
    slots, coupled, size = h_hbm.shape[3:6]
    side = 1 - 2 * (x % 2)
    lean = 1 - 2 * (y % 2)
    along_x = tuple((x + step * side + extent_x) % extent_x for step in (0, 1, -1, 2, -2))
    along_y = tuple((y + step * lean + extent_y) % extent_y for step in (0, -1, 1))
    along_z = tuple((z + step + extent_z) % extent_z for step in (0, 1, -1))
    inner = (z > 0) & (z < extent_z - 1)
    toward = jnp.where(z < extent_z // 2, 1, -1)

    def device(way):
        return along_x[way[0]], along_y[way[1]], along_z[way[2]]

    def single(way):
        return tuple(way[:2] + (step,) for step in ((UP, DOWN) if way[2] == BOTH else way[2:]))

    sends = FIRST_SENDS + SECOND_SENDS + sum((step[2] for step in ORDER if step[0] == SEND), ())
    ways = sorted({way for _, *rest in sends for way in single(tuple(rest))})
    back_x, back_z = (STAY, NEAR, FAR, BEHIND, AHEAD), (STAY, DOWN, UP)
    barrier = pltpu.get_barrier_semaphore()
    for way in ways:
        source = device((back_x[way[0]], way[1], back_z[way[2]]))
        pl.semaphore_signal(barrier, inc=1, device_id=source, device_id_type=MESH)

    load_counts = pltpu.make_async_copy(counts_hbm, counts, local_sem.at[0])
    load_raw = pltpu.make_async_copy(curr_hbm.at[0, 0, 0, 1], raw, local_sem.at[1])
    load_listed = pltpu.make_async_copy(listed_hbm, listed, local_sem.at[2])
    load_first = pltpu.make_async_copy(
        curr_hbm.at[0, 0, 0, 0], first.at[0, 0, OWN, 0], local_sem.at[3]
    )
    load_blocks = pltpu.make_async_copy(
        h_hbm.at[0, 0, 0], blocks.at[:, pl.ds(0, coupled)], local_sem.at[4]
    )
    load_prev = pltpu.make_async_copy(prev_hbm.at[0, 0, 0], prev, local_sem.at[5])
    load_density = pltpu.make_async_copy(density_hbm, density_ref, local_sem.at[6])
    load_coeffs = pltpu.make_async_copy(coeffs_hbm, coeffs, local_sem.at[7])
    for load in (
        load_counts,
        load_raw,
        load_listed,
        load_first,
        load_blocks,
        load_prev,
        load_density,
        load_coeffs,
    ):
        load.start()
    pl.semaphore_wait(barrier, len(ways))

    pending = []
    held = ((first, first_sem), (second, second_sem))

    def forward(step, block, sends, source=None):
        slot = block[0]
        ref, semaphores = held[slot]
        if source is None:
            source = ref.at[(step,) + block[1:]]
        when = inner if slot == 1 and block[1] == 0 else None
        for target, *rest in sends:
            at = (step,) + target[1:]
            for way in single(tuple(rest)):
                copy = pltpu.make_async_remote_copy(
                    src_ref=source,
                    dst_ref=ref.at[at],
                    send_sem=send_sem.at[len(pending)],
                    recv_sem=semaphores.at[at],
                    device_id=device(way),
                    device_id_type=MESH,
                )
                pending.append((copy, when))
                if when is None:
                    copy.start()
                else:
                    pl.when(when)(copy.start)

    def arrived(step, block):
        ref, semaphores = held[block[0]]
        at = (step,) + block[1:]
        copy = pltpu.make_async_remote_copy(
            src_ref=ref.at[at],
            dst_ref=ref.at[at],
            send_sem=send_sem.at[0],
            recv_sem=semaphores.at[at],
            device_id=device((STAY, PARTNER, STAY)),
            device_id_type=MESH,
        )
        if block[0] == 1 and block[1] == 0:
            pl.when(inner)(copy.wait_recv)
        else:
            copy.wait_recv()

    shift_x = (0, side, -side)
    shift_y = (0, -lean, lean)

    def add(step, slot, layer, column, start):
        shift_z = 0 if layer == 0 else toward if slot == 1 else 2 * layer - 3

        def multiply():
            rows = []
            for row in range(slots):
                parts = []
                for group in range(3):
                    offset = (shift_x[group] + 1) * 9 + (shift_y[column] + 1) * 3 + shift_z + 1
                    parts.append(blocks[row, place[row, offset * slots + slot]])
                rows.append(jnp.concatenate(parts, axis=1))
            product = jnp.dot(
                jnp.concatenate(rows, axis=0),
                held[slot][0][step, layer, column].reshape(3 * size, -1),
                preferred_element_type=jnp.float32,
            )
            total[...] = product if start else total[...] + product

        if slot == 1 and layer == 0:
            pl.when(inner)(multiply)
        else:
            multiply()

    def apply(step, before_first):
        started = False
        for kind, block, *rest in ORDER:
            if kind == WAIT:
                arrived(step, block)
            elif kind == SEND:
                own = curr_hbm.at[0, 0, 0, 0] if step == 0 and block == (0, 0, OWN, 0) else None
                forward(step, block, rest[0], own)
            else:
                if not started:
                    before_first()
                add(step, *block, not started)
                started = True

    forward(0, (0, 0, OWN, 0), FIRST_SENDS, curr_hbm.at[0, 0, 0, 0])
    load_counts.wait()
    load_raw.wait()
    live = counts[0, 0, 0] > 1
    second[0, 0, OWN, 0] = jnp.where(live, raw[...].astype(jnp.float32), 0.0).astype(raw.dtype)
    forward(0, (1, 0, OWN, 0), SECOND_SENDS)

    load_listed.wait()
    blocks[:, pl.ds(coupled, 1)] = jnp.zeros((slots, 1, size, size), blocks.dtype)
    lanes = lax.broadcasted_iota(jnp.int32, (1, place_rows.shape[1]), 1)
    for row in range(slots):
        found = jnp.full(lanes.shape, coupled, jnp.int32)
        for item in range(coupled):
            found = jnp.where(lanes == listed[0, 0, 0, row, item], item, found)
        place_rows[pl.ds(row, 1), :] = found
    load_place = pltpu.make_async_copy(place_rows, place, local_sem.at[8])
    load_place.start()
    load_first.wait()
    load_prev.wait()

    def before_first():
        load_place.wait()
        load_blocks.wait()

    apply(0, before_first)

    def product_less(row, before):
        value = 2.0 * total[pl.ds(row * size, size), :] - before.astype(jnp.float32)
        if row:
            value = jnp.where(live, value, 0.0)
        return value.astype(raw.dtype)

    mid = product_less(0, prev[0])
    first[1, 0, OWN, 0] = mid
    forward(1, (0, 0, OWN, 0), FIRST_SENDS)
    mid_ref[0, 0, 0, 0] = mid
    mid = product_less(1, prev[1])
    second[1, 0, OWN, 0] = mid
    forward(1, (1, 0, OWN, 0), SECOND_SENDS)
    mid_ref[0, 0, 0, 1] = mid

    load_density.wait()
    load_coeffs.wait()
    density_ref[...] += coeffs[0] * mid_ref[...].astype(jnp.float32)
    apply(1, lambda: None)
    for row in range(slots):
        value = product_less(row, held[row][0][0, 0, OWN, 0])
        next_ref[0, 0, 0, row] = value
        density_ref[0, 0, 0, row] += coeffs[1] * value.astype(jnp.float32)
    for copy, when in pending:
        if when is None:
            copy.wait_send()
        else:
            pl.when(when)(copy.wait_send)


def hand_over(*refs):
    count = len(refs) // 2
    sources, targets, semaphores = refs[:count], refs[count : 2 * count], refs[-1]
    copies = [
        pltpu.make_async_copy(source, target, semaphores.at[index])
        for index, (source, target) in enumerate(zip(sources, targets))
    ]
    for copy in copies:
        copy.start()
    for copy in copies:
        copy.wait()


def on_device(
    h_blocks, neighbours, block_counts, cheb_prev_in, cheb_curr_in, density_in, cheb_coeffs
):
    slots, coupled, size = h_blocks.shape[3:6]
    field = cheb_curr_in.shape
    probes = field[5]
    kind = cheb_curr_in.dtype
    in_hbm = pl.BlockSpec(memory_space=pltpu.HBM)
    in_vmem = pl.BlockSpec(memory_space=pltpu.VMEM)
    kept = functools.partial(pltpu.with_memory_space_constraint, memory_space=pltpu.HBM)
    results = (
        jax.ShapeDtypeStruct(field, kind),
        jax.ShapeDtypeStruct(field, kind),
        jax.ShapeDtypeStruct(field, jnp.float32),
    )
    made = pl.pallas_call(
        kernel,
        name="two_steps",
        out_shape=results,
        in_specs=[in_hbm] * 7,
        out_specs=(in_vmem,) * 3,
        scratch_shapes=[
            pltpu.VMEM((ROUNDS, 3, 3, 3, size, probes), kind),
            pltpu.VMEM((ROUNDS, 2, 3, 3, size, probes), kind),
            pltpu.VMEM((slots, coupled + 1, size, size), h_blocks.dtype),
            pltpu.VMEM((slots, size, probes), kind),
            pltpu.VMEM((size, probes), kind),
            pltpu.VMEM((slots * size, probes), jnp.float32),
            pltpu.VMEM((8, 128), jnp.int32),
            pltpu.SMEM((8, 128), jnp.int32),
            pltpu.SMEM(neighbours.shape, jnp.int32),
            pltpu.SMEM(block_counts.shape, jnp.int32),
            pltpu.SMEM(cheb_coeffs.shape, jnp.float32),
            pltpu.SemaphoreType.DMA((9,)),
            pltpu.SemaphoreType.DMA((ROUNDS * 64,)),
            pltpu.SemaphoreType.DMA((ROUNDS, 3, 3, 3)),
            pltpu.SemaphoreType.DMA((ROUNDS, 2, 3, 3)),
        ],
        compiler_params=pltpu.CompilerParams(
            collective_id=0, has_side_effects=True, vmem_limit_bytes=32 * 2**20
        ),
    )(
        kept(cheb_curr_in),
        kept(cheb_prev_in),
        kept(h_blocks),
        kept(neighbours),
        block_counts,
        kept(density_in),
        kept(cheb_coeffs),
    )
    return tuple(
        pl.pallas_call(
            hand_over,
            name="hand_over",
            out_shape=results,
            in_specs=[in_vmem] * 3,
            out_specs=(in_hbm,) * 3,
            scratch_shapes=[pltpu.SemaphoreType.DMA((3,))],
        )(*(pltpu.with_memory_space_constraint(array, pltpu.VMEM) for array in made))
    )


def solution(mesh):
    placed = (
        P("gx", "gy", "gz", None, None, None, None),
        P("gx", "gy", "gz", None, None),
        P("gx", "gy", "gz"),
        P("gx", "gy", "gz", None, None, None),
        P("gx", "gy", "gz", None, None, None),
        P("gx", "gy", "gz", None, None, None),
        P(),
    )
    return jax.shard_map(
        on_device,
        mesh=mesh,
        in_specs=placed,
        out_specs=(
            P("gx", "gy", "gz", None, None, None),
            P("gx", "gy", "gz", None, None, None),
            P("gx", "gy", "gz", None, None, None),
        ),
        check_vma=False,
    )
```

```python
import functools

import jax
import jax.numpy as jnp
from jax import lax
from jax.experimental import pallas as pl
from jax.experimental.pallas import tpu as pltpu
from jax.sharding import PartitionSpec as P

MESH = pl.DeviceIdType.MESH
ROUNDS = 2

OWN, CROSS, PARTNER = 0, 1, 2
STAY, NEAR, FAR, AHEAD, BEHIND = 0, 1, 2, 3, 4
UP, DOWN, BOTH = 1, 2, 3
WAIT, SEND, ADD = 0, 1, 2

FIRST_SENDS = (
    ((0, 0, 0, 2), FAR, OWN, STAY),
    ((0, 0, 0, 1), NEAR, OWN, STAY),
    ((0, 0, 1, 2), FAR, CROSS, STAY),
    ((0, 0, 1, 1), NEAR, CROSS, STAY),
    ((0, 0, 1, 0), STAY, CROSS, STAY),
    ((0, 1, 0, 0), STAY, OWN, UP),
    ((0, 2, 0, 0), STAY, OWN, DOWN),
    ((0, 0, 2, 0), STAY, PARTNER, STAY),
)
SECOND_SENDS = (
    ((1, 1, 0, 0), STAY, OWN, BOTH),
    ((1, 0, 0, 2), FAR, OWN, STAY),
    ((1, 0, 0, 1), NEAR, OWN, STAY),
    ((1, 0, 2, 0), STAY, PARTNER, STAY),
    ((1, 0, 1, 2), FAR, CROSS, STAY),
    ((1, 0, 1, 1), NEAR, CROSS, STAY),
    ((1, 0, 1, 0), STAY, CROSS, STAY),
)
ORDER = (
    (WAIT, (0, 0, 2, 0)),
    (WAIT, (1, 0, 2, 0)),
    (
        SEND,
        (1, 0, 2, 0),
        (
            ((1, 1, 2, 0), STAY, OWN, BOTH),
        ),
    ),
    (WAIT, (0, 1, 0, 0)),
    (WAIT, (0, 2, 0, 0)),
    (
        SEND,
        (0, 1, 0, 0),
        (
            ((0, 1, 2, 0), STAY, PARTNER, STAY),
        ),
    ),
    (
        SEND,
        (0, 2, 0, 0),
        (
            ((0, 2, 2, 0), STAY, PARTNER, STAY),
        ),
    ),
    (WAIT, (0, 0, 1, 0)),
    (
        SEND,
        (0, 0, 1, 0),
        (
            ((0, 1, 1, 0), STAY, OWN, UP),
            ((0, 2, 1, 0), STAY, OWN, DOWN),
        ),
    ),
    (WAIT, (1, 1, 0, 0)),
    (
        SEND,
        (1, 1, 0, 0),
        (
            ((1, 1, 0, 2), FAR, OWN, STAY),
            ((1, 1, 0, 1), NEAR, OWN, STAY),
            ((1, 1, 1, 2), FAR, CROSS, STAY),
            ((1, 1, 1, 1), NEAR, CROSS, STAY),
            ((1, 1, 1, 0), STAY, CROSS, STAY),
        ),
    ),
    (ADD, (0, 0, 0)),
    (WAIT, (0, 1, 2, 0)),
    (WAIT, (0, 2, 2, 0)),
    (WAIT, (0, 0, 0, 2)),
    (
        SEND,
        (0, 0, 0, 2),
        (
            ((0, 2, 0, 2), STAY, OWN, DOWN),
            ((0, 1, 0, 2), STAY, OWN, UP),
            ((0, 0, 2, 2), STAY, PARTNER, STAY),
        ),
    ),
    (WAIT, (0, 0, 0, 1)),
    (
        SEND,
        (0, 0, 0, 1),
        (
            ((0, 1, 0, 1), STAY, OWN, UP),
            ((0, 2, 0, 1), STAY, OWN, DOWN),
            ((0, 0, 2, 1), STAY, PARTNER, STAY),
        ),
    ),
    (WAIT, (0, 0, 1, 1)),
    (
        SEND,
        (0, 0, 1, 1),
        (
            ((0, 1, 1, 1), STAY, OWN, UP),
            ((0, 2, 1, 1), STAY, OWN, DOWN),
        ),
    ),
    (WAIT, (0, 0, 1, 2)),
    (
        SEND,
        (0, 0, 1, 2),
        (
            ((0, 1, 1, 2), STAY, OWN, UP),
            ((0, 2, 1, 2), STAY, OWN, DOWN),
        ),
    ),
    (WAIT, (1, 1, 2, 0)),
    (WAIT, (0, 0, 2, 2)),
    (WAIT, (0, 0, 2, 1)),
    (WAIT, (1, 0, 1, 0)),
    (ADD, (0, 0, 2)),
    (ADD, (0, 0, 1)),
    (WAIT, (1, 0, 0, 2)),
    (
        SEND,
        (1, 0, 0, 2),
        (
            ((1, 0, 2, 2), STAY, PARTNER, STAY),
        ),
    ),
    (WAIT, (1, 0, 0, 1)),
    (
        SEND,
        (1, 0, 0, 1),
        (
            ((1, 0, 2, 1), STAY, PARTNER, STAY),
        ),
    ),
    (WAIT, (1, 0, 1, 1)),
    (WAIT, (0, 1, 1, 0)),
    (WAIT, (0, 2, 1, 0)),
    (WAIT, (1, 0, 1, 2)),
    (ADD, (0, 1, 0)),
    (ADD, (0, 2, 0)),
    (WAIT, (1, 0, 2, 2)),
    (WAIT, (1, 1, 1, 0)),
    (ADD, (1, 0, 0)),
    (WAIT, (1, 0, 2, 1)),
    (WAIT, (0, 1, 0, 2)),
    (WAIT, (0, 2, 0, 2)),
    (
        SEND,
        (0, 1, 0, 2),
        (
            ((0, 1, 2, 2), STAY, PARTNER, STAY),
        ),
    ),
    (
        SEND,
        (0, 2, 0, 2),
        (
            ((0, 2, 2, 2), STAY, PARTNER, STAY),
        ),
    ),
    (ADD, (1, 0, 2)),
    (ADD, (1, 1, 0)),
    (ADD, (1, 0, 1)),
    (WAIT, (1, 1, 0, 1)),
    (
        SEND,
        (1, 1, 0, 1),
        (
            ((1, 1, 2, 1), STAY, PARTNER, STAY),
        ),
    ),
    (WAIT, (0, 1, 0, 1)),
    (WAIT, (0, 2, 0, 1)),
    (
        SEND,
        (0, 1, 0, 1),
        (
            ((0, 1, 2, 1), STAY, PARTNER, STAY),
        ),
    ),
    (
        SEND,
        (0, 2, 0, 1),
        (
            ((0, 2, 2, 1), STAY, PARTNER, STAY),
        ),
    ),
    (WAIT, (0, 2, 1, 1)),
    (WAIT, (1, 1, 0, 2)),
    (
        SEND,
        (1, 1, 0, 2),
        (
            ((1, 1, 2, 2), STAY, PARTNER, STAY),
        ),
    ),
    (WAIT, (0, 1, 2, 2)),
    (WAIT, (0, 2, 2, 2)),
    (WAIT, (0, 1, 1, 1)),
    (WAIT, (1, 1, 1, 1)),
    (WAIT, (0, 1, 2, 1)),
    (WAIT, (0, 2, 2, 1)),
    (WAIT, (1, 1, 1, 2)),
    (WAIT, (0, 1, 1, 2)),
    (WAIT, (0, 2, 1, 2)),
    (ADD, (0, 1, 1)),
    (ADD, (0, 1, 2)),
    (ADD, (0, 2, 2)),
    (WAIT, (1, 1, 2, 2)),
    (WAIT, (1, 1, 2, 1)),
    (ADD, (1, 1, 2)),
    (ADD, (1, 1, 1)),
    (ADD, (0, 2, 1)),
)


def kernel(
    curr_hbm,
    prev_hbm,
    h_hbm,
    listed_hbm,
    counts,
    density_hbm,
    coeffs_hbm,
    mid_ref,
    next_ref,
    density_ref,
    first,
    second,
    blocks,
    prev,
    raw,
    total,
    place_rows,
    place,
    listed,
    coeffs,
    local_sem,
    send_sem,
    first_sem,
    second_sem,
):
    extent_x, extent_y, extent_z = (lax.axis_size(a) for a in ("gx", "gy", "gz"))
    x, y, z = (lax.axis_index(a) for a in ("gx", "gy", "gz"))
    slots, coupled, size = h_hbm.shape[3:6]
    side = 1 - 2 * (x % 2)
    lean = 1 - 2 * (y % 2)
    along_x = tuple((x + step * side + extent_x) % extent_x for step in (0, 1, -1, 2, -2))
    along_y = tuple((y + step * lean + extent_y) % extent_y for step in (0, -1, 1))
    along_z = tuple((z + step + extent_z) % extent_z for step in (0, 1, -1))
    inner = (z > 0) & (z < extent_z - 1)
    toward = jnp.where(z < extent_z // 2, 1, -1)

    def device(way):
        return along_x[way[0]], along_y[way[1]], along_z[way[2]]

    def single(way):
        return tuple(way[:2] + (step,) for step in ((UP, DOWN) if way[2] == BOTH else way[2:]))

    sends = FIRST_SENDS + SECOND_SENDS + sum((step[2] for step in ORDER if step[0] == SEND), ())
    ways = sorted({way for _, *rest in sends for way in single(tuple(rest))})
    back_x, back_z = (STAY, NEAR, FAR, BEHIND, AHEAD), (STAY, DOWN, UP)
    barrier = pltpu.get_barrier_semaphore()
    for way in ways:
        source = device((back_x[way[0]], way[1], back_z[way[2]]))
        pl.semaphore_signal(barrier, inc=1, device_id=source, device_id_type=MESH)

    load_raw = pltpu.make_async_copy(curr_hbm.at[0, 0, 0, 1], raw, local_sem.at[1])
    load_listed = pltpu.make_async_copy(listed_hbm, listed, local_sem.at[2])
    load_first = pltpu.make_async_copy(
        curr_hbm.at[0, 0, 0, 0], first.at[0, 0, 0, OWN], local_sem.at[3]
    )
    load_blocks = pltpu.make_async_copy(
        h_hbm.at[0, 0, 0], blocks.at[:, pl.ds(0, coupled)], local_sem.at[4]
    )
    load_prev = pltpu.make_async_copy(prev_hbm.at[0, 0, 0], prev, local_sem.at[5])
    load_density = pltpu.make_async_copy(density_hbm, density_ref, local_sem.at[6])
    load_coeffs = pltpu.make_async_copy(coeffs_hbm, coeffs, local_sem.at[7])
    for load in (
        load_raw,
        load_listed,
        load_first,
        load_blocks,
        load_prev,
        load_density,
        load_coeffs,
    ):
        load.start()
    pl.semaphore_wait(barrier, len(ways))

    pending = []
    held = ((first, first_sem), (second, second_sem))

    def forward(step, block, sends, source=None):
        slot = block[0]
        ref, semaphores = held[slot]
        if source is None:
            source = ref.at[step, block[1], block[3], block[2]]
        when = inner if slot == 1 and block[1] == 0 else None
        copies = []
        for target, *rest in sends:
            at = (step, target[1], target[3], target[2])
            for way in single(tuple(rest)):
                copies.append(
                    pltpu.make_async_remote_copy(
                        src_ref=source,
                        dst_ref=ref.at[at],
                        send_sem=send_sem.at[len(pending)],
                        recv_sem=semaphores.at[at],
                        device_id=device(way),
                        device_id_type=MESH,
                    )
                )
                pending.append((copies[-1], when))

        def start():
            for copy in copies:
                copy.start()

        if when is None:
            start()
        else:
            pl.when(when)(start)

    def arrived(step, block):
        ref, semaphores = held[block[0]]
        at = (step, block[1], block[3], block[2])
        copy = pltpu.make_async_remote_copy(
            src_ref=ref.at[at],
            dst_ref=ref.at[at],
            send_sem=send_sem.at[0],
            recv_sem=semaphores.at[at],
            device_id=device((STAY, PARTNER, STAY)),
            device_id_type=MESH,
        )
        if block[0] == 1 and block[1] == 0:
            pl.when(inner)(copy.wait_recv)
        else:
            copy.wait_recv()

    shift_x = (0, side, -side)
    shift_y = (0, -lean, lean)

    def add(step, slot, layer, group, start):
        shift_z = 0 if layer == 0 else toward if slot == 1 else 2 * layer - 3

        def multiply():
            rows = []
            for row in range(slots):
                parts = []
                for column in range(3):
                    offset = (shift_x[group] + 1) * 9 + (shift_y[column] + 1) * 3 + shift_z + 1
                    parts.append(blocks[row, place[row, offset * slots + slot]])
                rows.append(jnp.concatenate(parts, axis=1))
            product = jnp.dot(
                jnp.concatenate(rows, axis=0),
                held[slot][0][step, layer, group].reshape(3 * size, -1),
                preferred_element_type=jnp.float32,
            )
            total[...] = product if start else total[...] + product

        if slot == 1 and layer == 0:
            pl.when(inner)(multiply)
        else:
            multiply()

    def apply(step, before_first):
        started = False
        for kind, block, *rest in ORDER:
            if kind == WAIT:
                arrived(step, block)
            elif kind == SEND:
                own = curr_hbm.at[0, 0, 0, 0] if step == 0 and block == (0, 0, OWN, 0) else None
                forward(step, block, rest[0], own)
            else:
                if not started:
                    before_first()
                add(step, *block, not started)
                started = True

    forward(0, (0, 0, OWN, 0), FIRST_SENDS, curr_hbm.at[0, 0, 0, 0])
    load_raw.wait()
    live = counts[0, 0, 0] > 1
    second[0, 0, 0, OWN] = jnp.where(live, raw[...].astype(jnp.float32), 0.0).astype(raw.dtype)
    forward(0, (1, 0, OWN, 0), SECOND_SENDS)

    load_listed.wait()
    blocks[:, pl.ds(coupled, 1)] = jnp.zeros((slots, 1, size, size), blocks.dtype)
    lanes = lax.broadcasted_iota(jnp.int32, (1, place_rows.shape[1]), 1)
    for row in range(slots):
        found = jnp.full(lanes.shape, coupled, jnp.int32)
        for item in range(coupled):
            found = jnp.where(lanes == listed[0, 0, 0, row, item], item, found)
        place_rows[pl.ds(row, 1), :] = found
    load_place = pltpu.make_async_copy(place_rows, place, local_sem.at[8])
    load_place.start()
    load_first.wait()
    load_prev.wait()

    def before_first():
        load_place.wait()
        load_blocks.wait()

    apply(0, before_first)

    def product_less(row, before):
        value = 2.0 * total[pl.ds(row * size, size), :] - before.astype(jnp.float32)
        if row:
            value = jnp.where(live, value, 0.0)
        return value.astype(raw.dtype)

    mid = product_less(0, prev[0])
    first[1, 0, 0, OWN] = mid
    forward(1, (0, 0, OWN, 0), FIRST_SENDS)
    mid_ref[0, 0, 0, 0] = mid
    mid = product_less(1, prev[1])
    second[1, 0, 0, OWN] = mid
    forward(1, (1, 0, OWN, 0), SECOND_SENDS)
    mid_ref[0, 0, 0, 1] = mid

    load_density.wait()
    load_coeffs.wait()
    density_ref[...] += coeffs[0] * mid_ref[...].astype(jnp.float32)
    apply(1, lambda: None)
    for row in range(slots):
        value = product_less(row, held[row][0][0, 0, 0, OWN])
        next_ref[0, 0, 0, row] = value
        density_ref[0, 0, 0, row] += coeffs[1] * value.astype(jnp.float32)
    for copy, when in pending:
        if when is None:
            copy.wait_send()

    @pl.when(inner)
    def _():
        for copy, when in pending:
            if when is not None:
                copy.wait_send()


def hand_over(*refs):
    count = len(refs) // 2
    sources, targets, semaphores = refs[:count], refs[count : 2 * count], refs[-1]
    copies = [
        pltpu.make_async_copy(source, target, semaphores.at[index])
        for index, (source, target) in enumerate(zip(sources, targets))
    ]
    for copy in copies:
        copy.start()
    for copy in copies:
        copy.wait()


def on_device(
    h_blocks, neighbours, block_counts, cheb_prev_in, cheb_curr_in, density_in, cheb_coeffs
):
    slots, coupled, size = h_blocks.shape[3:6]
    field = cheb_curr_in.shape
    probes = field[5]
    kind = cheb_curr_in.dtype
    in_hbm = pl.BlockSpec(memory_space=pltpu.HBM)
    in_smem = pl.BlockSpec(memory_space=pltpu.SMEM)
    in_vmem = pl.BlockSpec(memory_space=pltpu.VMEM)
    kept = functools.partial(pltpu.with_memory_space_constraint, memory_space=pltpu.HBM)
    results = (
        jax.ShapeDtypeStruct(field, kind),
        jax.ShapeDtypeStruct(field, kind),
        jax.ShapeDtypeStruct(field, jnp.float32),
    )
    made = pl.pallas_call(
        kernel,
        name="two_steps",
        out_shape=results,
        in_specs=[in_hbm] * 4 + [in_smem] + [in_hbm] * 2,
        out_specs=(in_vmem,) * 3,
        scratch_shapes=[
            pltpu.VMEM((ROUNDS, 3, 3, 3, size, probes), kind),
            pltpu.VMEM((ROUNDS, 2, 3, 3, size, probes), kind),
            pltpu.VMEM((slots, coupled + 1, size, size), h_blocks.dtype),
            pltpu.VMEM((slots, size, probes), kind),
            pltpu.VMEM((size, probes), kind),
            pltpu.VMEM((slots * size, probes), jnp.float32),
            pltpu.VMEM((8, 128), jnp.int32),
            pltpu.SMEM((8, 128), jnp.int32),
            pltpu.SMEM(neighbours.shape, jnp.int32),
            pltpu.SMEM(cheb_coeffs.shape, jnp.float32),
            pltpu.SemaphoreType.DMA((9,)),
            pltpu.SemaphoreType.DMA((ROUNDS * 64,)),
            pltpu.SemaphoreType.DMA((ROUNDS, 3, 3, 3)),
            pltpu.SemaphoreType.DMA((ROUNDS, 2, 3, 3)),
        ],
        compiler_params=pltpu.CompilerParams(
            collective_id=0, has_side_effects=True, vmem_limit_bytes=32 * 2**20
        ),
    )(
        kept(cheb_curr_in),
        kept(cheb_prev_in),
        kept(h_blocks),
        kept(neighbours),
        block_counts,
        kept(density_in),
        kept(cheb_coeffs),
    )
    return tuple(
        pl.pallas_call(
            hand_over,
            name="hand_over",
            out_shape=results,
            in_specs=[in_vmem] * 3,
            out_specs=(in_hbm,) * 3,
            scratch_shapes=[pltpu.SemaphoreType.DMA((3,))],
        )(*(pltpu.with_memory_space_constraint(array, pltpu.VMEM) for array in made))
    )


def solution(mesh):
    placed = (
        P("gx", "gy", "gz", None, None, None, None),
        P("gx", "gy", "gz", None, None),
        P("gx", "gy", "gz"),
        P("gx", "gy", "gz", None, None, None),
        P("gx", "gy", "gz", None, None, None),
        P("gx", "gy", "gz", None, None, None),
        P(),
    )
    return jax.shard_map(
        on_device,
        mesh=mesh,
        in_specs=placed,
        out_specs=(
            P("gx", "gy", "gz", None, None, None),
            P("gx", "gy", "gz", None, None, None),
            P("gx", "gy", "gz", None, None, None),
        ),
        check_vma=False,
    )
```

```python
import functools

import jax
import jax.numpy as jnp
from jax import lax
from jax.experimental import pallas as pl
from jax.experimental.pallas import tpu as pltpu
from jax.sharding import PartitionSpec as P

MESH = pl.DeviceIdType.MESH
ROUNDS = 2

OWN, CROSS, PARTNER = 0, 1, 2
STAY, NEAR, FAR, AHEAD, BEHIND = 0, 1, 2, 3, 4
UP, DOWN, BOTH = 1, 2, 3
WAIT, SEND, ADD = 0, 1, 2

FIRST_SENDS = (
    ((0, 0, 0, 2), FAR, OWN, STAY),
    ((0, 0, 0, 1), NEAR, OWN, STAY),
    ((0, 0, 1, 2), FAR, CROSS, STAY),
    ((0, 0, 1, 1), NEAR, CROSS, STAY),
    ((0, 0, 1, 0), STAY, CROSS, STAY),
    ((0, 1, 0, 0), STAY, OWN, UP),
    ((0, 2, 0, 0), STAY, OWN, DOWN),
    ((0, 0, 2, 0), STAY, PARTNER, STAY),
)
SECOND_SENDS = (
    ((1, 1, 0, 0), STAY, OWN, BOTH),
    ((1, 0, 0, 2), FAR, OWN, STAY),
    ((1, 0, 0, 1), NEAR, OWN, STAY),
    ((1, 0, 2, 0), STAY, PARTNER, STAY),
    ((1, 0, 1, 2), FAR, CROSS, STAY),
    ((1, 0, 1, 1), NEAR, CROSS, STAY),
    ((1, 0, 1, 0), STAY, CROSS, STAY),
)
ORDER = (
    (WAIT, (0, 0, 2, 0)),
    (WAIT, (1, 0, 2, 0)),
    (
        SEND,
        (1, 0, 2, 0),
        (
            ((1, 1, 2, 0), STAY, OWN, BOTH),
        ),
    ),
    (WAIT, (0, 1, 0, 0)),
    (WAIT, (0, 2, 0, 0)),
    (
        SEND,
        (0, 1, 0, 0),
        (
            ((0, 1, 2, 0), STAY, PARTNER, STAY),
        ),
    ),
    (
        SEND,
        (0, 2, 0, 0),
        (
            ((0, 2, 2, 0), STAY, PARTNER, STAY),
        ),
    ),
    (WAIT, (0, 0, 1, 0)),
    (
        SEND,
        (0, 0, 1, 0),
        (
            ((0, 1, 1, 0), STAY, OWN, UP),
            ((0, 2, 1, 0), STAY, OWN, DOWN),
        ),
    ),
    (WAIT, (1, 1, 0, 0)),
    (
        SEND,
        (1, 1, 0, 0),
        (
            ((1, 1, 0, 2), FAR, OWN, STAY),
            ((1, 1, 0, 1), NEAR, OWN, STAY),
            ((1, 1, 1, 2), FAR, CROSS, STAY),
            ((1, 1, 1, 1), NEAR, CROSS, STAY),
            ((1, 1, 1, 0), STAY, CROSS, STAY),
        ),
    ),
    (ADD, (0, 0, 0)),
    (WAIT, (0, 1, 2, 0)),
    (WAIT, (0, 2, 2, 0)),
    (WAIT, (0, 0, 0, 2)),
    (
        SEND,
        (0, 0, 0, 2),
        (
            ((0, 2, 0, 2), STAY, OWN, DOWN),
            ((0, 1, 0, 2), STAY, OWN, UP),
            ((0, 0, 2, 2), STAY, PARTNER, STAY),
        ),
    ),
    (WAIT, (0, 0, 0, 1)),
    (
        SEND,
        (0, 0, 0, 1),
        (
            ((0, 1, 0, 1), STAY, OWN, UP),
            ((0, 2, 0, 1), STAY, OWN, DOWN),
            ((0, 0, 2, 1), STAY, PARTNER, STAY),
        ),
    ),
    (WAIT, (0, 0, 1, 1)),
    (
        SEND,
        (0, 0, 1, 1),
        (
            ((0, 1, 1, 1), STAY, OWN, UP),
            ((0, 2, 1, 1), STAY, OWN, DOWN),
        ),
    ),
    (WAIT, (0, 0, 1, 2)),
    (
        SEND,
        (0, 0, 1, 2),
        (
            ((0, 1, 1, 2), STAY, OWN, UP),
            ((0, 2, 1, 2), STAY, OWN, DOWN),
        ),
    ),
    (WAIT, (1, 1, 2, 0)),
    (WAIT, (0, 0, 2, 2)),
    (WAIT, (0, 0, 2, 1)),
    (WAIT, (1, 0, 1, 0)),
    (ADD, (0, 0, 2)),
    (ADD, (0, 0, 1)),
    (WAIT, (1, 0, 0, 2)),
    (
        SEND,
        (1, 0, 0, 2),
        (
            ((1, 0, 2, 2), STAY, PARTNER, STAY),
        ),
    ),
    (WAIT, (1, 0, 0, 1)),
    (
        SEND,
        (1, 0, 0, 1),
        (
            ((1, 0, 2, 1), STAY, PARTNER, STAY),
        ),
    ),
    (WAIT, (1, 0, 1, 1)),
    (WAIT, (0, 1, 1, 0)),
    (WAIT, (0, 2, 1, 0)),
    (WAIT, (1, 0, 1, 2)),
    (ADD, (0, 1, 0)),
    (ADD, (0, 2, 0)),
    (WAIT, (1, 0, 2, 2)),
    (WAIT, (1, 1, 1, 0)),
    (ADD, (1, 0, 0)),
    (WAIT, (1, 0, 2, 1)),
    (WAIT, (0, 1, 0, 2)),
    (WAIT, (0, 2, 0, 2)),
    (
        SEND,
        (0, 1, 0, 2),
        (
            ((0, 1, 2, 2), STAY, PARTNER, STAY),
        ),
    ),
    (
        SEND,
        (0, 2, 0, 2),
        (
            ((0, 2, 2, 2), STAY, PARTNER, STAY),
        ),
    ),
    (ADD, (1, 0, 2)),
    (ADD, (1, 1, 0)),
    (ADD, (1, 0, 1)),
    (WAIT, (1, 1, 0, 1)),
    (
        SEND,
        (1, 1, 0, 1),
        (
            ((1, 1, 2, 1), STAY, PARTNER, STAY),
        ),
    ),
    (WAIT, (0, 1, 0, 1)),
    (WAIT, (0, 2, 0, 1)),
    (
        SEND,
        (0, 1, 0, 1),
        (
            ((0, 1, 2, 1), STAY, PARTNER, STAY),
        ),
    ),
    (
        SEND,
        (0, 2, 0, 1),
        (
            ((0, 2, 2, 1), STAY, PARTNER, STAY),
        ),
    ),
    (WAIT, (0, 2, 1, 1)),
    (WAIT, (1, 1, 0, 2)),
    (
        SEND,
        (1, 1, 0, 2),
        (
            ((1, 1, 2, 2), STAY, PARTNER, STAY),
        ),
    ),
    (WAIT, (0, 1, 2, 2)),
    (WAIT, (0, 2, 2, 2)),
    (WAIT, (0, 1, 1, 1)),
    (WAIT, (1, 1, 1, 1)),
    (WAIT, (0, 1, 2, 1)),
    (WAIT, (0, 2, 2, 1)),
    (WAIT, (1, 1, 1, 2)),
    (WAIT, (0, 1, 1, 2)),
    (WAIT, (0, 2, 1, 2)),
    (ADD, (0, 1, 1)),
    (ADD, (0, 1, 2)),
    (ADD, (0, 2, 2)),
    (WAIT, (1, 1, 2, 2)),
    (WAIT, (1, 1, 2, 1)),
    (ADD, (1, 1, 2)),
    (ADD, (1, 1, 1)),
    (ADD, (0, 2, 1)),
)


def kernel(
    curr_hbm,
    prev_hbm,
    h_hbm,
    listed_hbm,
    counts,
    density_hbm,
    coeffs_hbm,
    mid_ref,
    next_ref,
    density_ref,
    first,
    second,
    blocks,
    prev,
    raw,
    total,
    place_rows,
    place,
    listed,
    coeffs,
    local_sem,
    send_sem,
    first_sem,
    second_sem,
):
    extent_x, extent_y, extent_z = (lax.axis_size(a) for a in ("gx", "gy", "gz"))
    x, y, z = (lax.axis_index(a) for a in ("gx", "gy", "gz"))
    slots, coupled, size = h_hbm.shape[3:6]
    side = 1 - 2 * (x % 2)
    lean = 1 - 2 * (y % 2)
    along_x = tuple((x + step * side + extent_x) % extent_x for step in (0, 1, -1, 2, -2))
    along_y = tuple((y + step * lean + extent_y) % extent_y for step in (0, -1, 1))
    along_z = tuple((z + step + extent_z) % extent_z for step in (0, 1, -1))
    inner = (z > 0) & (z < extent_z - 1)
    toward = jnp.where(z < extent_z // 2, 1, -1)

    def device(way):
        return along_x[way[0]], along_y[way[1]], along_z[way[2]]

    def single(way):
        return tuple(way[:2] + (step,) for step in ((UP, DOWN) if way[2] == BOTH else way[2:]))

    sends = FIRST_SENDS + SECOND_SENDS + sum((step[2] for step in ORDER if step[0] == SEND), ())
    ways = sorted({way for _, *rest in sends for way in single(tuple(rest))})
    back_x, back_z = (STAY, NEAR, FAR, BEHIND, AHEAD), (STAY, DOWN, UP)
    barrier = pltpu.get_barrier_semaphore()
    for way in sorted(ways, key=lambda way: -sum(step != STAY for step in way)):
        source = device((back_x[way[0]], way[1], back_z[way[2]]))
        pl.semaphore_signal(barrier, inc=1, device_id=source, device_id_type=MESH)

    load_raw = pltpu.make_async_copy(curr_hbm.at[0, 0, 0, 1], raw, local_sem.at[1])
    load_listed = pltpu.make_async_copy(listed_hbm, listed, local_sem.at[2])
    load_first = pltpu.make_async_copy(
        curr_hbm.at[0, 0, 0, 0], first.at[0, 0, 0, OWN], local_sem.at[3]
    )
    load_blocks = pltpu.make_async_copy(
        h_hbm.at[0, 0, 0], blocks.at[:, pl.ds(0, coupled)], local_sem.at[4]
    )
    load_prev = pltpu.make_async_copy(prev_hbm.at[0, 0, 0], prev, local_sem.at[5])
    load_density = pltpu.make_async_copy(density_hbm, density_ref, local_sem.at[6])
    load_coeffs = pltpu.make_async_copy(coeffs_hbm, coeffs, local_sem.at[7])
    for load in (
        load_raw,
        load_listed,
        load_first,
        load_blocks,
        load_prev,
        load_density,
        load_coeffs,
    ):
        load.start()
    pl.semaphore_wait(barrier, len(ways))

    pending = []
    held = ((first, first_sem), (second, second_sem))

    def forward(step, block, sends, source=None):
        slot = block[0]
        ref, semaphores = held[slot]
        if source is None:
            source = ref.at[step, block[1], block[3], block[2]]
        when = inner if slot == 1 and block[1] == 0 else None
        copies = []
        for target, *rest in sends:
            at = (step, target[1], target[3], target[2])
            for way in single(tuple(rest)):
                copies.append(
                    pltpu.make_async_remote_copy(
                        src_ref=source,
                        dst_ref=ref.at[at],
                        send_sem=send_sem.at[len(pending)],
                        recv_sem=semaphores.at[at],
                        device_id=device(way),
                        device_id_type=MESH,
                    )
                )
                pending.append((copies[-1], when))

        def start():
            for copy in copies:
                copy.start()

        if when is None:
            start()
        else:
            pl.when(when)(start)

    def arrived(step, block):
        ref, semaphores = held[block[0]]
        at = (step, block[1], block[3], block[2])
        copy = pltpu.make_async_remote_copy(
            src_ref=ref.at[at],
            dst_ref=ref.at[at],
            send_sem=send_sem.at[0],
            recv_sem=semaphores.at[at],
            device_id=device((STAY, PARTNER, STAY)),
            device_id_type=MESH,
        )
        if block[0] == 1 and block[1] == 0:
            pl.when(inner)(copy.wait_recv)
        else:
            copy.wait_recv()

    shift_x = (0, side, -side)
    shift_y = (0, -lean, lean)

    def add(step, slot, layer, group, start):
        shift_z = 0 if layer == 0 else toward if slot == 1 else 2 * layer - 3

        def multiply():
            rows = []
            for row in range(slots):
                parts = []
                for column in range(3):
                    offset = (shift_x[group] + 1) * 9 + (shift_y[column] + 1) * 3 + shift_z + 1
                    parts.append(blocks[row, place[row, offset * slots + slot]])
                rows.append(jnp.concatenate(parts, axis=1))
            product = jnp.dot(
                jnp.concatenate(rows, axis=0),
                held[slot][0][step, layer, group].reshape(3 * size, -1),
                preferred_element_type=jnp.float32,
            )
            total[...] = product if start else total[...] + product

        if slot == 1 and layer == 0:
            pl.when(inner)(multiply)
        else:
            multiply()

    def apply(step, before_first):
        started = False
        for kind, block, *rest in ORDER:
            if kind == WAIT:
                arrived(step, block)
            elif kind == SEND:
                own = curr_hbm.at[0, 0, 0, 0] if step == 0 and block == (0, 0, OWN, 0) else None
                forward(step, block, rest[0], own)
            else:
                if not started:
                    before_first()
                add(step, *block, not started)
                started = True

    forward(0, (0, 0, OWN, 0), FIRST_SENDS, curr_hbm.at[0, 0, 0, 0])
    load_raw.wait()
    live = counts[0, 0, 0] > 1
    second[0, 0, 0, OWN] = jnp.where(live, raw[...].astype(jnp.float32), 0.0).astype(raw.dtype)
    forward(0, (1, 0, OWN, 0), SECOND_SENDS)

    load_listed.wait()
    blocks[:, pl.ds(coupled, 1)] = jnp.zeros((slots, 1, size, size), blocks.dtype)
    lanes = lax.broadcasted_iota(jnp.int32, (1, place_rows.shape[1]), 1)
    for row in range(slots):
        found = jnp.full(lanes.shape, coupled, jnp.int32)
        for item in range(coupled):
            found = jnp.where(lanes == listed[0, 0, 0, row, item], item, found)
        place_rows[pl.ds(row, 1), :] = found
    load_place = pltpu.make_async_copy(place_rows, place, local_sem.at[8])
    load_place.start()
    load_first.wait()
    load_prev.wait()

    def before_first():
        load_place.wait()
        load_blocks.wait()

    apply(0, before_first)

    def product_less(row, before):
        value = 2.0 * total[pl.ds(row * size, size), :] - before.astype(jnp.float32)
        if row:
            value = jnp.where(live, value, 0.0)
        return value.astype(raw.dtype)

    mid = product_less(0, prev[0])
    first[1, 0, 0, OWN] = mid
    forward(1, (0, 0, OWN, 0), FIRST_SENDS)
    mid_ref[0, 0, 0, 0] = mid
    mid = product_less(1, prev[1])
    second[1, 0, 0, OWN] = mid
    forward(1, (1, 0, OWN, 0), SECOND_SENDS)
    mid_ref[0, 0, 0, 1] = mid

    load_density.wait()
    load_coeffs.wait()
    density_ref[...] += coeffs[0] * mid_ref[...].astype(jnp.float32)
    apply(1, lambda: None)
    for row in range(slots):
        value = product_less(row, held[row][0][0, 0, 0, OWN])
        next_ref[0, 0, 0, row] = value
        density_ref[0, 0, 0, row] += coeffs[1] * value.astype(jnp.float32)
    for copy, when in pending:
        if when is None:
            copy.wait_send()

    @pl.when(inner)
    def _():
        for copy, when in pending:
            if when is not None:
                copy.wait_send()


def hand_over(*refs):
    count = len(refs) // 2
    sources, targets, semaphores = refs[:count], refs[count : 2 * count], refs[-1]
    copies = [
        pltpu.make_async_copy(source, target, semaphores.at[index])
        for index, (source, target) in enumerate(zip(sources, targets))
    ]
    for copy in copies:
        copy.start()
    for copy in copies:
        copy.wait()


def on_device(
    h_blocks, neighbours, block_counts, cheb_prev_in, cheb_curr_in, density_in, cheb_coeffs
):
    slots, coupled, size = h_blocks.shape[3:6]
    field = cheb_curr_in.shape
    probes = field[5]
    kind = cheb_curr_in.dtype
    in_hbm = pl.BlockSpec(memory_space=pltpu.HBM)
    in_smem = pl.BlockSpec(memory_space=pltpu.SMEM)
    in_vmem = pl.BlockSpec(memory_space=pltpu.VMEM)
    kept = functools.partial(pltpu.with_memory_space_constraint, memory_space=pltpu.HBM)
    results = (
        jax.ShapeDtypeStruct(field, kind),
        jax.ShapeDtypeStruct(field, kind),
        jax.ShapeDtypeStruct(field, jnp.float32),
    )
    made = pl.pallas_call(
        kernel,
        name="two_steps",
        out_shape=results,
        in_specs=[in_hbm] * 4 + [in_smem] + [in_hbm] * 2,
        out_specs=(in_vmem,) * 3,
        scratch_shapes=[
            pltpu.VMEM((ROUNDS, 3, 3, 3, size, probes), kind),
            pltpu.VMEM((ROUNDS, 2, 3, 3, size, probes), kind),
            pltpu.VMEM((slots, coupled + 1, size, size), h_blocks.dtype),
            pltpu.VMEM((slots, size, probes), kind),
            pltpu.VMEM((size, probes), kind),
            pltpu.VMEM((slots * size, probes), jnp.float32),
            pltpu.VMEM((8, 128), jnp.int32),
            pltpu.SMEM((8, 128), jnp.int32),
            pltpu.SMEM(neighbours.shape, jnp.int32),
            pltpu.SMEM(cheb_coeffs.shape, jnp.float32),
            pltpu.SemaphoreType.DMA((9,)),
            pltpu.SemaphoreType.DMA((ROUNDS * 64,)),
            pltpu.SemaphoreType.DMA((ROUNDS, 3, 3, 3)),
            pltpu.SemaphoreType.DMA((ROUNDS, 2, 3, 3)),
        ],
        compiler_params=pltpu.CompilerParams(
            collective_id=0, has_side_effects=True, vmem_limit_bytes=32 * 2**20
        ),
    )(
        kept(cheb_curr_in),
        kept(cheb_prev_in),
        kept(h_blocks),
        kept(neighbours),
        block_counts,
        kept(density_in),
        kept(cheb_coeffs),
    )
    return tuple(
        pl.pallas_call(
            hand_over,
            name="hand_over",
            out_shape=results,
            in_specs=[in_vmem] * 3,
            out_specs=(in_hbm,) * 3,
            scratch_shapes=[pltpu.SemaphoreType.DMA((3,))],
        )(*(pltpu.with_memory_space_constraint(array, pltpu.VMEM) for array in made))
    )


def solution(mesh):
    placed = (
        P("gx", "gy", "gz", None, None, None, None),
        P("gx", "gy", "gz", None, None),
        P("gx", "gy", "gz"),
        P("gx", "gy", "gz", None, None, None),
        P("gx", "gy", "gz", None, None, None),
        P("gx", "gy", "gz", None, None, None),
        P(),
    )
    return jax.shard_map(
        on_device,
        mesh=mesh,
        in_specs=placed,
        out_specs=(
            P("gx", "gy", "gz", None, None, None),
            P("gx", "gy", "gz", None, None, None),
            P("gx", "gy", "gz", None, None, None),
        ),
        check_vma=False,
    )
```

```python
import functools

import jax
import jax.numpy as jnp
from jax import lax
from jax.experimental import pallas as pl
from jax.experimental.pallas import tpu as pltpu
from jax.sharding import PartitionSpec as P

MESH = pl.DeviceIdType.MESH
ROUNDS = 2

OWN, CROSS, PARTNER = 0, 1, 2
STAY, NEAR, FAR, AHEAD, BEHIND = 0, 1, 2, 3, 4
UP, DOWN, BOTH = 1, 2, 3
WAIT, SEND, ADD = 0, 1, 2

FIRST_SENDS = (
    ((0, 0, 0, 2), FAR, OWN, STAY),
    ((0, 0, 0, 1), NEAR, OWN, STAY),
    ((0, 0, 1, 2), FAR, CROSS, STAY),
    ((0, 0, 1, 1), NEAR, CROSS, STAY),
    ((0, 0, 1, 0), STAY, CROSS, STAY),
    ((0, 1, 0, 0), STAY, OWN, UP),
    ((0, 2, 0, 0), STAY, OWN, DOWN),
    ((0, 0, 2, 0), STAY, PARTNER, STAY),
)
SECOND_SENDS = (
    ((1, 1, 0, 0), STAY, OWN, BOTH),
    ((1, 0, 0, 2), FAR, OWN, STAY),
    ((1, 0, 0, 1), NEAR, OWN, STAY),
    ((1, 0, 1, 2), FAR, CROSS, STAY),
    ((1, 0, 1, 1), NEAR, CROSS, STAY),
    ((1, 0, 1, 0), STAY, CROSS, STAY),
    ((1, 0, 2, 0), STAY, PARTNER, STAY),
)
ORDER = (
    (WAIT, (0, 0, 2, 0)),
    (WAIT, (1, 0, 2, 0)),
    (WAIT, (0, 1, 0, 0)),
    (WAIT, (0, 2, 0, 0)),
    (
        SEND,
        (0, 1, 0, 0),
        (
            ((0, 1, 2, 0), STAY, PARTNER, STAY),
        ),
    ),
    (
        SEND,
        (0, 2, 0, 0),
        (
            ((0, 2, 2, 0), STAY, PARTNER, STAY),
        ),
    ),
    (WAIT, (0, 0, 1, 0)),
    (
        SEND,
        (0, 0, 1, 0),
        (
            ((0, 1, 1, 0), STAY, OWN, UP),
            ((0, 2, 1, 0), STAY, OWN, DOWN),
        ),
    ),
    (WAIT, (1, 1, 0, 0)),
    (
        SEND,
        (1, 1, 0, 0),
        (
            ((1, 1, 0, 2), FAR, OWN, STAY),
            ((1, 1, 0, 1), NEAR, OWN, STAY),
            ((1, 1, 1, 2), FAR, CROSS, STAY),
            ((1, 1, 1, 1), NEAR, CROSS, STAY),
            ((1, 1, 1, 0), STAY, CROSS, STAY),
            ((1, 1, 2, 0), STAY, PARTNER, STAY),
        ),
    ),
    (ADD, (0, 0, 0)),
    (WAIT, (0, 1, 2, 0)),
    (WAIT, (0, 2, 2, 0)),
    (WAIT, (0, 0, 0, 2)),
    (
        SEND,
        (0, 0, 0, 2),
        (
            ((0, 1, 0, 2), STAY, OWN, UP),
            ((0, 2, 0, 2), STAY, OWN, DOWN),
            ((0, 0, 2, 2), STAY, PARTNER, STAY),
        ),
    ),
    (WAIT, (0, 0, 0, 1)),
    (
        SEND,
        (0, 0, 0, 1),
        (
            ((0, 1, 0, 1), STAY, OWN, UP),
            ((0, 2, 0, 1), STAY, OWN, DOWN),
            ((0, 0, 2, 1), STAY, PARTNER, STAY),
        ),
    ),
    (WAIT, (0, 0, 1, 1)),
    (
        SEND,
        (0, 0, 1, 1),
        (
            ((0, 1, 1, 1), STAY, OWN, UP),
            ((0, 2, 1, 1), STAY, OWN, DOWN),
        ),
    ),
    (WAIT, (0, 0, 1, 2)),
    (
        SEND,
        (0, 0, 1, 2),
        (
            ((0, 1, 1, 2), STAY, OWN, UP),
            ((0, 2, 1, 2), STAY, OWN, DOWN),
        ),
    ),
    (WAIT, (1, 1, 2, 0)),
    (WAIT, (0, 0, 2, 2)),
    (WAIT, (0, 0, 2, 1)),
    (WAIT, (1, 0, 1, 0)),
    (ADD, (0, 0, 2)),
    (ADD, (0, 0, 1)),
    (ADD, (1, 0, 0)),
    (WAIT, (1, 0, 0, 2)),
    (
        SEND,
        (1, 0, 0, 2),
        (
            ((1, 0, 2, 2), STAY, PARTNER, STAY),
        ),
    ),
    (WAIT, (1, 0, 0, 1)),
    (
        SEND,
        (1, 0, 0, 1),
        (
            ((1, 0, 2, 1), STAY, PARTNER, STAY),
        ),
    ),
    (WAIT, (1, 0, 1, 1)),
    (WAIT, (0, 1, 1, 0)),
    (WAIT, (0, 2, 1, 0)),
    (WAIT, (1, 0, 1, 2)),
    (ADD, (0, 1, 0)),
    (ADD, (0, 2, 0)),
    (WAIT, (1, 0, 2, 2)),
    (WAIT, (1, 1, 1, 0)),
    (WAIT, (1, 0, 2, 1)),
    (WAIT, (0, 1, 0, 2)),
    (WAIT, (0, 2, 0, 2)),
    (
        SEND,
        (0, 1, 0, 2),
        (
            ((0, 1, 2, 2), STAY, PARTNER, STAY),
        ),
    ),
    (
        SEND,
        (0, 2, 0, 2),
        (
            ((0, 2, 2, 2), STAY, PARTNER, STAY),
        ),
    ),
    (ADD, (1, 0, 2)),
    (ADD, (1, 1, 0)),
    (ADD, (1, 0, 1)),
    (WAIT, (1, 1, 0, 1)),
    (
        SEND,
        (1, 1, 0, 1),
        (
            ((1, 1, 2, 1), STAY, PARTNER, STAY),
        ),
    ),
    (WAIT, (0, 1, 0, 1)),
    (WAIT, (0, 2, 0, 1)),
    (
        SEND,
        (0, 1, 0, 1),
        (
            ((0, 1, 2, 1), STAY, PARTNER, STAY),
        ),
    ),
    (
        SEND,
        (0, 2, 0, 1),
        (
            ((0, 2, 2, 1), STAY, PARTNER, STAY),
        ),
    ),
    (WAIT, (0, 2, 1, 1)),
    (WAIT, (1, 1, 0, 2)),
    (
        SEND,
        (1, 1, 0, 2),
        (
            ((1, 1, 2, 2), STAY, PARTNER, STAY),
        ),
    ),
    (WAIT, (0, 1, 2, 2)),
    (WAIT, (0, 2, 2, 2)),
    (WAIT, (0, 1, 1, 1)),
    (WAIT, (1, 1, 1, 1)),
    (WAIT, (0, 1, 2, 1)),
    (WAIT, (0, 2, 2, 1)),
    (WAIT, (1, 1, 1, 2)),
    (WAIT, (0, 1, 1, 2)),
    (WAIT, (0, 2, 1, 2)),
    (ADD, (0, 1, 1)),
    (ADD, (0, 2, 1)),
    (ADD, (0, 1, 2)),
    (ADD, (0, 2, 2)),
    (WAIT, (1, 1, 2, 2)),
    (WAIT, (1, 1, 2, 1)),
    (ADD, (1, 1, 2)),
    (ADD, (1, 1, 1)),
)


def kernel(
    curr_hbm,
    prev_hbm,
    h_hbm,
    listed_hbm,
    counts,
    density_hbm,
    coeffs_hbm,
    mid_ref,
    next_ref,
    density_ref,
    first,
    second,
    blocks,
    prev,
    raw,
    total,
    place_rows,
    place,
    listed,
    coeffs,
    local_sem,
    send_sem,
    first_sem,
    second_sem,
):
    extent_x, extent_y, extent_z = (lax.axis_size(a) for a in ("gx", "gy", "gz"))
    x, y, z = (lax.axis_index(a) for a in ("gx", "gy", "gz"))
    slots, coupled, size = h_hbm.shape[3:6]
    side = 1 - 2 * (x % 2)
    lean = 1 - 2 * (y % 2)
    along_x = tuple((x + step * side + extent_x) % extent_x for step in (0, 1, -1, 2, -2))
    along_y = tuple((y + step * lean + extent_y) % extent_y for step in (0, -1, 1))
    along_z = tuple((z + step + extent_z) % extent_z for step in (0, 1, -1))
    inner = (z > 0) & (z < extent_z - 1)
    toward = jnp.where(z < extent_z // 2, 1, -1)

    def device(way):
        return along_x[way[0]], along_y[way[1]], along_z[way[2]]

    def single(way):
        return tuple(way[:2] + (step,) for step in ((UP, DOWN) if way[2] == BOTH else way[2:]))

    sends = FIRST_SENDS + SECOND_SENDS + sum((step[2] for step in ORDER if step[0] == SEND), ())
    ways = sorted({way for _, *rest in sends for way in single(tuple(rest))})
    back_x, back_z = (STAY, NEAR, FAR, BEHIND, AHEAD), (STAY, DOWN, UP)
    barrier = pltpu.get_barrier_semaphore()
    for way in sorted(ways, key=lambda way: -sum(step != STAY for step in way)):
        source = device((back_x[way[0]], way[1], back_z[way[2]]))
        pl.semaphore_signal(barrier, inc=1, device_id=source, device_id_type=MESH)

    load_raw = pltpu.make_async_copy(curr_hbm.at[0, 0, 0, 1], raw, local_sem.at[1])
    load_listed = pltpu.make_async_copy(listed_hbm, listed, local_sem.at[2])
    load_first = pltpu.make_async_copy(
        curr_hbm.at[0, 0, 0, 0], first.at[0, 0, 0, OWN], local_sem.at[3]
    )
    load_blocks = pltpu.make_async_copy(
        h_hbm.at[0, 0, 0], blocks.at[:, pl.ds(0, coupled)], local_sem.at[4]
    )
    load_prev = pltpu.make_async_copy(prev_hbm.at[0, 0, 0], prev, local_sem.at[5])
    load_density = pltpu.make_async_copy(density_hbm, density_ref, local_sem.at[6])
    load_coeffs = pltpu.make_async_copy(coeffs_hbm, coeffs, local_sem.at[7])
    for load in (
        load_raw,
        load_listed,
        load_first,
        load_blocks,
        load_prev,
        load_density,
        load_coeffs,
    ):
        load.start()
    pl.semaphore_wait(barrier, len(ways))

    pending = []
    held = ((first, first_sem), (second, second_sem))

    def forward(step, block, sends, source=None):
        slot = block[0]
        ref, semaphores = held[slot]
        if source is None:
            source = ref.at[step, block[1], block[3], block[2]]
        when = inner if slot == 1 and block[1] == 0 else None
        copies = []
        for target, *rest in sends:
            at = (step, target[1], target[3], target[2])
            for way in single(tuple(rest)):
                copies.append(
                    pltpu.make_async_remote_copy(
                        src_ref=source,
                        dst_ref=ref.at[at],
                        send_sem=send_sem.at[len(pending)],
                        recv_sem=semaphores.at[at],
                        device_id=device(way),
                        device_id_type=MESH,
                    )
                )
                pending.append((copies[-1], when))

        def start():
            for copy in copies:
                copy.start()

        if when is None:
            start()
        else:
            pl.when(when)(start)

    def arrived(step, block):
        ref, semaphores = held[block[0]]
        at = (step, block[1], block[3], block[2])
        copy = pltpu.make_async_remote_copy(
            src_ref=ref.at[at],
            dst_ref=ref.at[at],
            send_sem=send_sem.at[0],
            recv_sem=semaphores.at[at],
            device_id=device((STAY, PARTNER, STAY)),
            device_id_type=MESH,
        )
        if block[0] == 1 and block[1] == 0:
            pl.when(inner)(copy.wait_recv)
        else:
            copy.wait_recv()

    shift_x = (0, side, -side)
    shift_y = (0, -lean, lean)

    def add(step, slot, layer, group, start):
        shift_z = 0 if layer == 0 else toward if slot == 1 else 2 * layer - 3

        def multiply():
            rows = []
            for row in range(slots):
                parts = []
                for column in range(3):
                    offset = (shift_x[group] + 1) * 9 + (shift_y[column] + 1) * 3 + shift_z + 1
                    parts.append(blocks[row, place[row, offset * slots + slot]])
                rows.append(jnp.concatenate(parts, axis=1))
            product = jnp.dot(
                jnp.concatenate(rows, axis=0),
                held[slot][0][step, layer, group].reshape(3 * size, -1),
                preferred_element_type=jnp.float32,
            )
            total[...] = product if start else total[...] + product

        if slot == 1 and layer == 0:
            pl.when(inner)(multiply)
        else:
            multiply()

    def apply(step, before_first):
        started = False
        for kind, block, *rest in ORDER:
            if kind == WAIT:
                arrived(step, block)
            elif kind == SEND:
                own = curr_hbm.at[0, 0, 0, 0] if step == 0 and block == (0, 0, OWN, 0) else None
                forward(step, block, rest[0], own)
            else:
                if not started:
                    before_first()
                add(step, *block, not started)
                started = True

    forward(0, (0, 0, OWN, 0), FIRST_SENDS, curr_hbm.at[0, 0, 0, 0])
    load_raw.wait()
    live = counts[0, 0, 0] > 1
    second[0, 0, 0, OWN] = jnp.where(live, raw[...].astype(jnp.float32), 0.0).astype(raw.dtype)
    forward(0, (1, 0, OWN, 0), SECOND_SENDS)

    load_listed.wait()
    blocks[:, pl.ds(coupled, 1)] = jnp.zeros((slots, 1, size, size), blocks.dtype)
    lanes = lax.broadcasted_iota(jnp.int32, (1, place_rows.shape[1]), 1)
    for row in range(slots):
        found = jnp.full(lanes.shape, coupled, jnp.int32)
        for item in range(coupled):
            found = jnp.where(lanes == listed[0, 0, 0, row, item], item, found)
        place_rows[pl.ds(row, 1), :] = found
    load_place = pltpu.make_async_copy(place_rows, place, local_sem.at[8])
    load_place.start()
    load_first.wait()
    load_prev.wait()

    def before_first():
        load_place.wait()
        load_blocks.wait()

    apply(0, before_first)

    def product_less(row, before):
        value = 2.0 * total[pl.ds(row * size, size), :] - before.astype(jnp.float32)
        if row:
            value = jnp.where(live, value, 0.0)
        return value.astype(raw.dtype)

    mid = product_less(0, prev[0])
    first[1, 0, 0, OWN] = mid
    forward(1, (0, 0, OWN, 0), FIRST_SENDS)
    mid_ref[0, 0, 0, 0] = mid
    mid = product_less(1, prev[1])
    second[1, 0, 0, OWN] = mid
    forward(1, (1, 0, OWN, 0), SECOND_SENDS)
    mid_ref[0, 0, 0, 1] = mid

    load_density.wait()
    load_coeffs.wait()
    density_ref[...] += coeffs[0] * mid_ref[...].astype(jnp.float32)
    apply(1, lambda: None)
    for row in range(slots):
        value = product_less(row, held[row][0][0, 0, 0, OWN])
        next_ref[0, 0, 0, row] = value
        density_ref[0, 0, 0, row] += coeffs[1] * value.astype(jnp.float32)
    for copy, when in pending:
        if when is None:
            copy.wait_send()

    @pl.when(inner)
    def _():
        for copy, when in pending:
            if when is not None:
                copy.wait_send()


def hand_over(*refs):
    count = len(refs) // 2
    sources, targets, semaphores = refs[:count], refs[count : 2 * count], refs[-1]
    copies = [
        pltpu.make_async_copy(source, target, semaphores.at[index])
        for index, (source, target) in enumerate(zip(sources, targets))
    ]
    for copy in copies:
        copy.start()
    for copy in copies:
        copy.wait()


def on_device(
    h_blocks, neighbours, block_counts, cheb_prev_in, cheb_curr_in, density_in, cheb_coeffs
):
    slots, coupled, size = h_blocks.shape[3:6]
    field = cheb_curr_in.shape
    probes = field[5]
    kind = cheb_curr_in.dtype
    in_hbm = pl.BlockSpec(memory_space=pltpu.HBM)
    in_smem = pl.BlockSpec(memory_space=pltpu.SMEM)
    in_vmem = pl.BlockSpec(memory_space=pltpu.VMEM)
    kept = functools.partial(pltpu.with_memory_space_constraint, memory_space=pltpu.HBM)
    results = (
        jax.ShapeDtypeStruct(field, kind),
        jax.ShapeDtypeStruct(field, kind),
        jax.ShapeDtypeStruct(field, jnp.float32),
    )
    made = pl.pallas_call(
        kernel,
        name="two_steps",
        out_shape=results,
        in_specs=[in_hbm] * 4 + [in_smem] + [in_hbm] * 2,
        out_specs=(in_vmem,) * 3,
        scratch_shapes=[
            pltpu.VMEM((ROUNDS, 3, 3, 3, size, probes), kind),
            pltpu.VMEM((ROUNDS, 2, 3, 3, size, probes), kind),
            pltpu.VMEM((slots, coupled + 1, size, size), h_blocks.dtype),
            pltpu.VMEM((slots, size, probes), kind),
            pltpu.VMEM((size, probes), kind),
            pltpu.VMEM((slots * size, probes), jnp.float32),
            pltpu.VMEM((8, 128), jnp.int32),
            pltpu.SMEM((8, 128), jnp.int32),
            pltpu.SMEM(neighbours.shape, jnp.int32),
            pltpu.SMEM(cheb_coeffs.shape, jnp.float32),
            pltpu.SemaphoreType.DMA((9,)),
            pltpu.SemaphoreType.DMA((ROUNDS * 64,)),
            pltpu.SemaphoreType.DMA((ROUNDS, 3, 3, 3)),
            pltpu.SemaphoreType.DMA((ROUNDS, 2, 3, 3)),
        ],
        compiler_params=pltpu.CompilerParams(
            collective_id=0, has_side_effects=True, vmem_limit_bytes=32 * 2**20
        ),
    )(
        kept(cheb_curr_in),
        kept(cheb_prev_in),
        kept(h_blocks),
        kept(neighbours),
        block_counts,
        kept(density_in),
        kept(cheb_coeffs),
    )
    return tuple(
        pl.pallas_call(
            hand_over,
            name="hand_over",
            out_shape=results,
            in_specs=[in_vmem] * 3,
            out_specs=(in_hbm,) * 3,
            scratch_shapes=[pltpu.SemaphoreType.DMA((3,))],
        )(*(pltpu.with_memory_space_constraint(array, pltpu.VMEM) for array in made))
    )


def solution(mesh):
    placed = (
        P("gx", "gy", "gz", None, None, None, None),
        P("gx", "gy", "gz", None, None),
        P("gx", "gy", "gz"),
        P("gx", "gy", "gz", None, None, None),
        P("gx", "gy", "gz", None, None, None),
        P("gx", "gy", "gz", None, None, None),
        P(),
    )
    return jax.shard_map(
        on_device,
        mesh=mesh,
        in_specs=placed,
        out_specs=(
            P("gx", "gy", "gz", None, None, None),
            P("gx", "gy", "gz", None, None, None),
            P("gx", "gy", "gz", None, None, None),
        ),
        check_vma=False,
    )
```
